32 devices in a mesh: seq: 4 (over x, core), grp: 4 (over z), head: 2 (over y).
Axes of the slice: x: 2, y: 2, z: 4, core: 2. Of those that a mesh axis runs over, the one named last changes fastest.
Arguments:
- query_feat: bfloat16 [4, 4, 512, 6144], P('grp', 'seq', None, 'head'), may hold values from -6 to 6
- key_feat: bfloat16 [4, 4, 512, 6144], P('grp', 'seq', None, 'head'), may hold values from -6 to 6
- value_feat: bfloat16 [4, 4, 512, 6144], P('grp', 'seq', None, 'head'), may hold values from -6 to 6
- norm_gain: float32 [6144], P('head'), may hold values from 0.5 to 1.5
Outputs:
- attended: bfloat16 [4, 4, 512, 6144], P('grp', 'seq', None, 'head')
The draws below stay inside these ranges and needn't reach their ends.
All inputs are finite; a program needn't handle non-finite values.
Results may differ from the reference program's by a relative error of at most 0.0049.
Values sent between devices are 32-bit elements; how exact they have to be, the bound alone decides.
No kernel may reach another device: no remote copies, remote signals or barrier semaphores. Data moves between devices by JAX's collectives and lax.ppermute only.
A program may use at most 128 MiB of HBM per device.

```python
import jax
import jax.numpy as jnp
from jax import lax

HEADS = 48
DH = 128
BLK = 512
TOK_DEV = 512
GROUPS = 4
SHARDS = 4


def levels(stream_key, dims, pieces, smallest, high):
    def one(position, parts):
        draws = jax.random.uniform(jax.random.fold_in(jax.random.fold_in(stream_key, 6), position), (parts,), jnp.float32, smallest / len(pieces), high / len(pieces))
        return jnp.repeat(jnp.exp(draws), dims[position] // parts).reshape((-1,) + (1,) * (len(dims) - position - 1))

    loudness = one(*pieces[0])
    for cut in pieces[1:]:
        loudness = loudness * one(*cut)
    return loudness


def normal_values(rng, extent, spread, reach, pieces=(), held_as=jnp.bfloat16):
    entries = jax.random.normal(rng, extent, jnp.float32) * spread
    if len(pieces) > 0:
        entries = levels(rng, extent, pieces, -0.22, 0.18) * entries
    return jnp.clip(entries, min=-reach, max=reach).astype(held_as)


def setup_inputs(seed: int = 0) -> dict:
    splits = jax.random.split(jax.random.key(seed), 5)
    return {
        "query_feat": normal_values(splits[0], (GROUPS, SHARDS, TOK_DEV, HEADS * DH), 1.0, 6.0, ((0, 4), (1, 4), (3, 2))),
        "key_feat": normal_values(splits[1], (GROUPS, SHARDS, TOK_DEV, HEADS * DH), 1.0, 6.0, ((0, 4), (1, 4), (3, 2))),
        "value_feat": normal_values(splits[2], (GROUPS, SHARDS, TOK_DEV, HEADS * DH), 1.0, 6.0, ((0, 4), (1, 4), (3, 2))),
        "norm_gain": jnp.clip(1.0 + 0.1 * jax.random.normal(splits[3], (HEADS * DH,), jnp.float32), 0.5, 1.5),
    }


def reference(query_feat, key_feat, value_feat, norm_gain):
    total = GROUPS * SHARDS * TOK_DEV
    nblocks = total // BLK

    def split(array):
        return array.reshape(nblocks, BLK, HEADS, DH)
    causal = jnp.arange(BLK)[:, None] >= jnp.arange(BLK)[None, :]
    gain = norm_gain.astype(jnp.float32).reshape(HEADS, DH)

    def advance(state, block):
        queries, keys_in, values = block
        q_wide = queries.astype(jnp.float32)
        k_wide = keys_in.astype(jnp.float32)
        v_wide = values.astype(jnp.float32)
        scores = jnp.einsum('thd,shd->hts', q_wide, k_wide)
        scores = jnp.where(causal[None], scores, 0.0)
        scores = lax.optimization_barrier(scores.astype(jnp.bfloat16)).astype(jnp.float32)
        rounded = lax.optimization_barrier(state.astype(jnp.bfloat16)).astype(jnp.float32)
        mixed = jnp.einsum('hts,she->the', scores, v_wide) + jnp.einsum('thd,hde->the', q_wide, rounded)
        meansq = lax.optimization_barrier(jnp.mean(mixed * mixed, axis=-1, keepdims=True))
        result = (mixed * lax.rsqrt(meansq + 1e-05) * gain).astype(jnp.bfloat16)
        new_state = state + jnp.einsum('thd,the->hde', k_wide, v_wide)
        return (new_state, result)
    start = jnp.zeros((HEADS, DH, DH), jnp.float32)
    _, outputs = lax.scan(advance, start, (split(query_feat), split(key_feat), split(value_feat)))
    return outputs.reshape(GROUPS, SHARDS, TOK_DEV, HEADS * DH)
```

```python
import functools

import jax
import jax.numpy as jnp
from jax import lax
from jax.experimental import pallas as pl
from jax.experimental.pallas import tpu as pltpu
from jax.sharding import PartitionSpec as P

DH = 128
BLK = 512
TILE = 256
CHUNKS = 2
F32 = jnp.float32
BF16 = jnp.bfloat16
VMEM_LIMIT = 48 * 1024 * 1024


def params():
    return pltpu.CompilerParams(vmem_limit_bytes=VMEM_LIMIT)


def head_cols(i):
    return slice(i * DH, (i + 1) * DH)


def kvsum_block(heads, k_ref, v_ref, write):
    for i in range(heads):
        total = lax.dot_general(
            k_ref[:, head_cols(i)],
            v_ref[:, head_cols(i)],
            (((0,), (0,)), ((), ())),
            preferred_element_type=F32,
        )
        write(i, total)


def kvsum_kernel(heads, where_ref, k_ref, v_ref, keep_ref, send_ref):
    step = pl.program_id(0)

    @pl.when(step < 2)
    def _():
        def write(i, total):
            keep_ref[0, head_cols(i), :] = total

        kvsum_block(heads, k_ref, v_ref, write)

    @pl.when(step >= 2)
    def _():
        def write(i, total):
            send_ref[0, head_cols(i), :] = total

        kvsum_block(heads, k_ref, v_ref, write)


def slot_block(chunk, step, where):
    half = (step // 2) ^ where[0]
    quarter = (step % 2) ^ where[1]
    return chunk * 4 + half * 2 + quarter


def kvsum_chunk(where, k, v, chunk, heads):
    tokens = k.shape[0]
    width = heads * DH

    def columns(step, where_ref):
        return (0, slot_block(chunk, step, where_ref))

    return pl.pallas_call(
        functools.partial(kvsum_kernel, heads),
        grid_spec=pltpu.PrefetchScalarGridSpec(
            num_scalar_prefetch=1,
            grid=(4,),
            in_specs=[pl.BlockSpec((tokens, width), columns)] * 2,
            out_specs=[
                pl.BlockSpec((1, width, DH), lambda s, w: (jnp.minimum(s, 1), 0, 0)),
                pl.BlockSpec((1, width, DH), lambda s, w: (jnp.maximum(s - 2, 0), 0, 0)),
            ],
        ),
        out_shape=[jax.ShapeDtypeStruct((2, width, DH), F32)] * 2,
        compiler_params=params(),
        cost_estimate=pl.CostEstimate(
            flops=8 * heads * tokens * DH * DH,
            bytes_accessed=16 * tokens * width + 16 * width * DH,
            transcendentals=0,
        ),
        name="kvsum",
    )(where, k, v)


def local_kernel(heads, q_ref, k_ref, v_ref, mixed_ref):
    rows = lax.broadcasted_iota(jnp.int32, (TILE, TILE), 0)
    cols = lax.broadcasted_iota(jnp.int32, (TILE, TILE), 1)
    causal = rows >= cols
    for i in range(heads):
        c = head_cols(i)
        for t in range(BLK // TILE):
            at = slice(t * TILE, (t + 1) * TILE)
            total = None
            for s in range(t + 1):
                seen = slice(s * TILE, (s + 1) * TILE)
                scores = lax.dot_general(
                    q_ref[at, c], k_ref[seen, c], (((1,), (1,)), ((), ())), preferred_element_type=F32
                )
                if s == t:
                    scores = jnp.where(causal, scores, 0.0)
                part = jnp.dot(scores.astype(BF16), v_ref[seen, c], preferred_element_type=F32)
                total = part if total is None else total + part
            mixed_ref[at, c] = total


def local_chunk(q, k, v, chunk, count, heads):
    tokens = q.shape[0]
    nblocks = tokens // BLK
    steps = count // heads
    width = heads * DH
    spec = pl.BlockSpec((BLK, width), lambda b, s: (b, chunk * steps + s))
    return pl.pallas_call(
        functools.partial(local_kernel, heads),
        grid=(nblocks, steps),
        in_specs=[spec] * 3,
        out_specs=pl.BlockSpec((BLK, width), lambda b, s: (b, s)),
        out_shape=jax.ShapeDtypeStruct((tokens, count * DH), F32),
        compiler_params=params(),
        cost_estimate=pl.CostEstimate(
            flops=3 * count * tokens * BLK * DH,
            bytes_accessed=10 * tokens * count * DH,
            transcendentals=0,
        ),
        name="local_attention",
    )(q, k, v)


def finish_head(q, state, mixed, gain):
    mixed = mixed + jnp.dot(q, state.astype(BF16), preferred_element_type=F32)
    meansq = jnp.mean(mixed * mixed, axis=-1, keepdims=True)
    return (mixed * lax.rsqrt(meansq + 1e-05) * gain).astype(BF16)


def finish_kernel(heads, first, where_ref, q_ref, mixed_ref, gain_ref, own_ref, add_ref, other_ref, *rest):
    out_ref = rest[-1]
    step = pl.program_id(0)
    scale = where_ref[0].astype(F32)

    def run(state_of):
        for i in range(heads):
            c = head_cols(i)
            out_ref[:, c] = finish_head(q_ref[:, c], state_of(c), mixed_ref[:, c], gain_ref[:, c])

    @pl.when(step < 2)
    def _():
        run(lambda c: own_ref[0, c, :] + scale * add_ref[0, c, :])

    @pl.when(step >= 2)
    def _():
        run(lambda c: other_ref[0, c, :])


def finish_chunk(where, q, mixed, gain, own, add, other, out, chunk, heads):
    tokens, total = q.shape
    width = heads * DH

    def columns(step, where_ref):
        return (0, slot_block(chunk, step, where_ref))

    def local_columns(step, where_ref):
        return (0, slot_block(0, step, where_ref))

    kept = pl.BlockSpec((1, width, DH), lambda s, w: (jnp.minimum(s, 1), 0, 0))
    in_specs = [
        pl.BlockSpec((tokens, width), columns),
        pl.BlockSpec((tokens, width), local_columns),
        pl.BlockSpec((1, width), columns),
        kept,
        kept,
        pl.BlockSpec((1, width, DH), lambda s, w: (jnp.maximum(s - 2, 0), 0, 0)),
    ]
    operands = [q, mixed, gain, own, add, other]
    aliases = {}
    if out is not None:
        in_specs.append(pl.BlockSpec(memory_space=pl.ANY))
        operands.append(out)
        aliases = {7: 0}
    return pl.pallas_call(
        functools.partial(finish_kernel, heads, out is None),
        grid_spec=pltpu.PrefetchScalarGridSpec(
            num_scalar_prefetch=1,
            grid=(4,),
            in_specs=in_specs,
            out_specs=pl.BlockSpec((tokens, width), columns),
        ),
        out_shape=jax.ShapeDtypeStruct((tokens, total), BF16),
        input_output_aliases=aliases,
        compiler_params=params(),
        cost_estimate=pl.CostEstimate(
            flops=8 * heads * tokens * DH * DH,
            bytes_accessed=32 * tokens * width,
            transcendentals=0,
        ),
        name="finish",
    )(where, *operands)


def fast_path(q, k, v, gain, groups, heads_here):
    chunks = range(CHUNKS)
    heads = heads_here // (4 * CHUNKS)
    position = lax.axis_index("seq")
    core, chip = position % 2, position // 2
    where = jnp.stack([core, chip]).astype(jnp.int32)
    second_core, second_chip = core.astype(F32), chip.astype(F32)
    other_core = [(0, 1), (1, 0), (2, 3), (3, 2)]
    other_chip = [(0, 2), (2, 0), (1, 3), (3, 1)]

    kept, sent = zip(*[kvsum_chunk(where, k, v, j, heads) for j in chunks])
    from_core = [lax.ppermute(s, "seq", other_core) for s in sent]
    sums = [a + b for a, b in zip(kept, from_core)]
    here = [s[0] for s in sums]
    there = [s[1] for s in sums]
    mixed = [None] * CHUNKS

    there[-1], held = lax.optimization_barrier((there[-1], q))
    first_mixed = local_chunk(held, k, v, 0, 4 * heads, heads)
    from_chip = [lax.ppermute(s, "seq", other_chip) for s in there]
    from_chip[0], mixed[0] = lax.optimization_barrier((from_chip[0], first_mixed))
    group_total = [a + b for a, b in zip(here, from_chip)]
    group_total[-1], held = lax.optimization_barrier((group_total[-1], q))
    later_mixed = [local_chunk(held, k, v, j, 4 * heads, heads) for j in chunks[1:]]

    arrived = [[] for _ in chunks]
    passing = group_total
    for hop in range(groups - 1):
        received = [lax.ppermute(p, "grp", [(hop, hop + 1)]) for p in passing]
        if hop == 0:
            received[0], mixed[1:] = lax.optimization_barrier((received[0], later_mixed))
        for j in chunks:
            arrived[j].append(received[j])
        passing = [r + g for r, g in zip(received, group_total)]
    before = [sum(a) if a else jnp.zeros_like(g) for a, g in zip(arrived, group_total)]

    back = [b + (1.0 - second_chip) * h for b, h in zip(before, here)]
    from_chip_back = [lax.ppermute(b, "seq", other_chip) for b in back]
    mine = [
        jnp.stack([b + second_chip * c, r])
        for b, c, r in zip(before, from_chip, from_chip_back)
    ]
    back = [m + (1.0 - second_core) * a for m, a in zip(mine, kept)]
    from_core_back = [lax.ppermute(b, "seq", other_core) for b in back]

    out = None
    for j in chunks:
        out = finish_chunk(
            where, q, mixed[j], gain, mine[j], from_core[j], from_core_back[j], out, j, heads
        )
    return out


def general_states(k, v, heads_here, nblocks, groups):
    def split(array):
        return array.reshape(nblocks, BLK, heads_here, DH)

    block_sums = jnp.einsum("bthd,bthe->bhde", split(k), split(v), preferred_element_type=F32)
    total = jnp.sum(block_sums, axis=0)
    earlier = jnp.concatenate([jnp.zeros_like(total)[None], jnp.cumsum(block_sums, axis=0)[:-1]])
    gathered = lax.all_gather(total, "seq")
    position = lax.axis_index("seq")
    lower = lax.broadcasted_iota(jnp.int32, (gathered.shape[0], 1, 1, 1), 0) < position
    within = jnp.sum(jnp.where(lower, gathered, 0.0), axis=0)
    group_total = jnp.sum(gathered, axis=0)
    before = jnp.zeros_like(total)
    passing = group_total
    for hop in range(groups - 1):
        received = lax.ppermute(passing, "grp", [(hop, hop + 1)])
        before = before + received
        passing = received + group_total
    return (before + within)[None] + earlier


def general_path(q, k, v, gain, groups, heads_here):
    tokens = q.shape[0]
    nblocks = tokens // BLK
    states = general_states(k, v, heads_here, nblocks, groups).astype(BF16)
    mixed = local_chunk(q, k, v, 0, heads_here, 1).reshape(nblocks, BLK, heads_here, DH)
    queries = q.reshape(nblocks, BLK, heads_here, DH)
    mixed = mixed + jnp.einsum("bthd,bhde->bthe", queries, states, preferred_element_type=F32)
    meansq = jnp.mean(mixed * mixed, axis=-1, keepdims=True)
    result = mixed * lax.rsqrt(meansq + 1e-05) * gain.reshape(heads_here, DH)
    return result.astype(BF16).reshape(q.shape)


def per_device(groups, shards, query_feat, key_feat, value_feat, norm_gain):
    shape = query_feat.shape
    tokens, width = shape[2:]
    heads_here = width // DH
    q, k, v = (a.reshape(tokens, width) for a in (query_feat, key_feat, value_feat))
    gain = norm_gain.reshape(1, width)
    fits = shards == 4 and tokens == BLK and heads_here % (4 * CHUNKS) == 0
    path = fast_path if fits else general_path
    return path(q, k, v, gain, groups, heads_here).reshape(shape)


def solution(mesh):
    placed = P("grp", "seq", None, "head")
    return jax.shard_map(
        functools.partial(per_device, mesh.shape["grp"], mesh.shape["seq"]),
        mesh=mesh,
        in_specs=(placed, placed, placed, P("head")),
        out_specs=placed,
        check_vma=False,
    )
```

```python
import functools

import jax
import jax.numpy as jnp
from jax import lax
from jax.experimental import pallas as pl
from jax.experimental.pallas import tpu as pltpu
from jax.sharding import PartitionSpec as P

DH = 128
BLK = 512
TILE = 256
CHUNKS = 2
EARLY = 3
SMALL = pl.CostEstimate(flops=1000, bytes_accessed=0, transcendentals=0)
F32 = jnp.float32
BF16 = jnp.bfloat16
VMEM_LIMIT = 8 * 1024 * 1024


def params():
    return pltpu.CompilerParams(vmem_limit_bytes=VMEM_LIMIT)


def in_hbm(array):
    return pltpu.with_memory_space_constraint(array, pltpu.HBM)


def in_vmem(array):
    return pltpu.with_memory_space_constraint(array, pltpu.VMEM)


def head_cols(i):
    return slice(i * DH, (i + 1) * DH)


def slot_column(slot, width, core, chip):
    half = (slot // 2) ^ core
    quarter = (slot % 2) ^ chip
    return pl.multiple_of((half * 2 + quarter) * width, DH)


class Slots:
    def __init__(self, where_ref, width):
        self.core, self.chip, self.width = where_ref[0], where_ref[1], width

    def column(self, first, slot):
        return pl.multiple_of(first + slot_column(slot, self.width, self.core, self.chip), DH)

    def load(self, first, slot, source, target, sem):
        copy = pltpu.make_async_copy(
            source.at[:, pl.ds(self.column(first, slot), self.width)], target, sem
        )
        copy.start()
        return copy


def specs(*spaces):
    return [pl.BlockSpec(memory_space=s) for s in spaces]


SLOT_ORDER = (3, 2, 0, 1)
KVSUM_OUTS = 6


def kvsum_kernel(width, where_ref, k_hbm, v_hbm, q_hbm, *refs):
    *refs, q_ref, sems = refs
    slots = Slots(where_ref, width)
    outs = [refs[KVSUM_OUTS * j : KVSUM_OUTS * (j + 1)] for j in range(CHUNKS)]
    loads = []
    for slot in SLOT_ORDER:
        for j in range(CHUNKS):
            k_ref, v_ref = outs[j][4:]
            first = 4 * width * j
            loads.append(
                (
                    slot,
                    j,
                    slots.load(first, slot, k_hbm, k_ref.at[slot], sems.at[0, j, slot]),
                    slots.load(first, slot, v_hbm, v_ref.at[slot], sems.at[1, j, slot]),
                )
            )
    q_load = slots.load(0, 0, q_hbm, q_ref, sems.at[2, 0, 0])
    for slot, j, *copies in loads:
        for copy in copies:
            copy.wait()
        lead, rest, own, other, k_ref, v_ref = outs[j]
        for i in range(width // DH):
            c = head_cols(i)
            total = lax.dot_general(
                k_ref[slot, :, c],
                v_ref[slot, :, c],
                (((0,), (0,)), ((), ())),
                preferred_element_type=F32,
            )
            if slot == 3:
                lead[c, :] = total
            else:
                rest[(slot + 1) % 3, c, :] = total
            if slot < 2:
                (own, other)[slot][c, :] = total
    q_load.wait()


def kvsum(where, q, k, v, width):
    tokens = k.shape[0]
    one = pltpu.VMEM((width, DH), F32)
    part = pltpu.VMEM((4, tokens, width), BF16)
    outs = [one, pltpu.VMEM((3, width, DH), F32), one, one, part, part] * CHUNKS
    outs.append(pltpu.VMEM((tokens, width), BF16))
    results = pl.pallas_call(
        functools.partial(kvsum_kernel, width),
        in_specs=specs(pltpu.SMEM, *[pltpu.HBM] * 3),
        out_specs=specs(*[pltpu.VMEM] * len(outs)),
        out_shape=outs,
        scratch_shapes=[pltpu.SemaphoreType.DMA((3, CHUNKS, 4))],
        compiler_params=params(),
        cost_estimate=SMALL,
        name="kvsum",
    )(where, in_hbm(k), in_hbm(v), in_hbm(q))
    return [results[KVSUM_OUTS * j : KVSUM_OUTS * (j + 1)] for j in range(CHUNKS)], results[-1]


def local_scores(q_ref, k_ref, c):
    rows = lax.broadcasted_iota(jnp.int32, (TILE, TILE), 0)
    cols = lax.broadcasted_iota(jnp.int32, (TILE, TILE), 1)
    causal = rows >= cols
    tiles = []
    for t in range(BLK // TILE):
        scores = lax.dot_general(
            q_ref[t * TILE : (t + 1) * TILE, c],
            k_ref[: (t + 1) * TILE, c],
            (((1,), (1,)), ((), ())),
            preferred_element_type=F32,
        )
        last = jnp.where(causal, scores[:, t * TILE :], 0.0).astype(BF16)
        if t > 0:
            last = jnp.concatenate([scores[:, : t * TILE].astype(BF16), last], axis=1)
        tiles.append(last)
    return tiles


def local_mix(tiles, v_ref, out_ref, c):
    for t, scores in enumerate(tiles):
        out_ref[t * TILE : (t + 1) * TILE, c] = jnp.dot(
            scores, v_ref[: (t + 1) * TILE, c], preferred_element_type=F32
        )


def local_heads(items):
    held = None
    for q_ref, k_ref, v_ref, out_ref, c in items:
        tiles = local_scores(q_ref, k_ref, c)
        if held is not None:
            local_mix(*held)
        held = (tiles, v_ref, out_ref, c)
    local_mix(*held)


def local_kernel(heads, q_ref, k_ref, v_ref, mixed_ref):
    local_heads([(q_ref, k_ref, v_ref, mixed_ref, head_cols(i)) for i in range(heads)])


def local_blocks(q, k, v, heads):
    tokens, width = q.shape
    spec = pl.BlockSpec((BLK, heads * DH), lambda b, s: (b, s))
    return pl.pallas_call(
        functools.partial(local_kernel, heads),
        grid=(tokens // BLK, width // (heads * DH)),
        in_specs=[spec] * 3,
        out_specs=spec,
        out_shape=jax.ShapeDtypeStruct((tokens, width), F32),
        compiler_params=params(),
        name="local_attention",
    )(q, k, v)


def local_slots_kernel(width, places, where_ref, q_hbm, *refs):
    count = len(places)
    if q_hbm is None:
        q_refs, loads = dict(zip(places, refs)), {}
        refs = refs[count:]
    else:
        every = [(j, n) for j in range(CHUNKS) for n in range(4)]
        *refs, sems = refs
        q_refs = dict(zip(every, [refs[0], *refs[-len(every) + 1 :]]))
        refs = refs[1:]
        slots = Slots(where_ref, width)
        loads = {
            (j, n): slots.load(4 * width * j, n, q_hbm, q_refs[j, n], sems.at[j, n])
            for j, n in every[1:]
        }
    k_refs, v_refs, out_refs = refs[:CHUNKS], refs[CHUNKS : 2 * CHUNKS], refs[2 * CHUNKS :]

    def items():
        for place, out_ref in zip(places, out_refs):
            j, n = place
            if place in loads:
                loads.pop(place).wait()
            for i in range(width // DH):
                yield q_refs[place], k_refs[j].at[n], v_refs[j].at[n], out_ref, head_cols(i)

    local_heads(items())
    for copy in loads.values():
        copy.wait()


def local_slots(where, q, q_lead, q_slots, k_parts, v_parts, width, places):
    tokens = k_parts[0].shape[1]
    first = q_lead is not None
    every = 4 * CHUNKS
    kernel = functools.partial(local_slots_kernel, width, places)
    if not first:
        kernel = lambda where_ref, *refs: local_slots_kernel(width, places, where_ref, None, *refs)
    queries = [q_lead] if first else [q_slots[p] for p in places]
    outs = [pltpu.VMEM((tokens, width), F32)] * len(places)
    outs += [pltpu.VMEM((tokens, width), BF16)] * ((every - 1) * first)
    results = pl.pallas_call(
        kernel,
        in_specs=specs(
            pltpu.SMEM, *[pltpu.HBM] * first, *[pltpu.VMEM] * (len(queries) + 2 * CHUNKS)
        ),
        out_specs=specs(*[pltpu.VMEM] * len(outs)),
        out_shape=outs,
        scratch_shapes=[pltpu.SemaphoreType.DMA((CHUNKS, 4))] * first,
        compiler_params=params(),
        cost_estimate=SMALL,
        name="local_attention",
    )(where, *([in_hbm(q)] if first else []), *[in_vmem(a) for a in (*queries, *k_parts, *v_parts)])
    return results[: len(places)], results[len(places) :]


def finish_kernel(first, width, where_ref, gain_ref, *refs):
    q_refs, mixed_refs = refs[:4], refs[4:8]
    own_near, own_far, lead_ref, rest_ref, far_near, far_far = refs[8:14]
    out_hbm, out_ref, sems = refs[-3:]
    slots = Slots(where_ref, width)
    second = slots.core.astype(F32)
    states = (own_near, own_far, far_near, far_far)
    from_core = (rest_ref.at[0], lead_ref, rest_ref.at[1], rest_ref.at[2])
    stores = []
    for n in range(4):
        column = slots.column(first, n)
        for i in range(width // DH):
            c = head_cols(i)
            state = states[n][c, :] + second * from_core[n][c, :]
            mixed = mixed_refs[n][:, c] + jnp.dot(
                q_refs[n][:, c], state.astype(BF16), preferred_element_type=F32
            )
            meansq = jnp.mean(mixed * mixed, axis=-1, keepdims=True)
            gain = gain_ref[:, pl.ds(pl.multiple_of(column + i * DH, DH), DH)]
            out_ref[n, :, c] = (mixed * lax.rsqrt(meansq + 1e-05) * gain).astype(BF16)
        store = pltpu.make_async_copy(out_ref.at[n], out_hbm.at[:, pl.ds(column, width)], sems.at[n])
        store.start()
        stores.append(store)
    for store in stores:
        store.wait()


def finish(where, gain, queries, mixed, states, out, first, width):
    tokens = queries[0].shape[0]
    earlier = [] if out is None else [out]
    operands = [where, gain, *[in_vmem(a) for a in (*queries, *mixed)], *states]
    return pl.pallas_call(
        functools.partial(finish_kernel, first, width),
        in_specs=specs(pltpu.SMEM, *[pltpu.VMEM] * (len(operands) - 1), *[pltpu.HBM] * len(earlier)),
        out_specs=specs(pltpu.HBM)[0],
        out_shape=jax.ShapeDtypeStruct((tokens, gain.shape[1]), BF16),
        scratch_shapes=[pltpu.VMEM((4, tokens, width), BF16), pltpu.SemaphoreType.DMA((4,))],
        input_output_aliases={len(operands): 0} if earlier else {},
        compiler_params=params(),
        cost_estimate=SMALL,
        name="finish",
    )(*operands, *earlier)


def combine(compute, count, where, *operands):
    shape = operands[0].shape

    def kernel(where_ref, *refs):
        ins, outs = refs[: len(operands)], refs[len(operands) :]
        core, chip = where_ref[0].astype(F32), where_ref[1].astype(F32)
        results = compute(core, chip, *[r[...] for r in ins])
        for ref, value in zip(outs, results):
            ref[...] = value

    return pl.pallas_call(
        kernel,
        in_specs=specs(pltpu.SMEM, *[pltpu.VMEM] * len(operands)),
        out_specs=specs(*[pltpu.VMEM] * count),
        out_shape=[jax.ShapeDtypeStruct(shape, F32)] * count,
        compiler_params=params(),
        cost_estimate=SMALL,
        name="combine",
    )(where, *operands)


def tie(*values):
    return lax.optimization_barrier(values)


def fast_path(q, k, v, gain, groups, heads_here):
    chunks = range(CHUNKS)
    width = heads_here // (4 * CHUNKS) * DH
    position = lax.axis_index("seq")
    core, chip = position % 2, position // 2
    where = jnp.stack([core, chip]).astype(jnp.int32)
    other_core = [(0, 1), (1, 0), (2, 3), (3, 2)]
    other_chip = [(0, 2), (2, 0), (1, 3), (3, 1)]

    sums, q_lead = kvsum(where, q, k, v, width)
    lead = [lax.ppermute(s[0], "seq", other_core) for s in sums]
    there = [s[3] + r for s, r in zip(sums, lead)]
    rest = [lax.ppermute(s[1], "seq", other_core) for s in sums]
    k_parts, v_parts = [s[4] for s in sums], [s[5] for s in sums]
    every = [(j, n) for j in chunks for n in range(4)]
    there[0], held = tie(there[0], where)
    early, q_slots = local_slots(held, q, q_lead, None, k_parts, v_parts, width, every[:EARLY])
    q_slots = dict(zip(every, [q_lead, *q_slots]))
    *later_there, early = tie(*there[1:], early)
    there[1:] = later_there
    from_chip = [lax.ppermute(t, "seq", other_chip) for t in there]
    here = [s[2] + r[0] for s, r in zip(sums, rest)]
    first_total, held = tie(here[0] + from_chip[0], where)
    late, _ = local_slots(held, None, None, q_slots, k_parts, v_parts, width, every[EARLY:])
    *later_chip, late = tie(*from_chip[1:], late)
    from_chip[1:] = later_chip
    group_total = [first_total] + [h + r for h, r in zip(here[1:], from_chip[1:])]
    local = dict(zip(every, [*early, *late]))

    arrived = [[] for _ in chunks]
    passing = group_total
    for hop in range(groups - 1):
        received = [lax.ppermute(p, "grp", [(hop, hop + 1)]) for p in passing]
        for j in chunks:
            arrived[j].append(received[j])
        passing = [r + g for r, g in zip(received, group_total)]

    def turn(core, chip, here, from_chip, *arrived):
        before = sum(arrived[1:], arrived[0])
        return before + (1.0 - chip) * here, before + chip * from_chip

    turned = [combine(turn, 2, where, here[j], from_chip[j], *arrived[j]) for j in chunks]
    from_chip_back = [lax.ppermute(back, "seq", other_chip) for back, _ in turned]
    near_back = [lax.ppermute(own, "seq", other_core) for _, own in turned]
    out = None
    for j in chunks:
        if out is not None:
            from_chip_back[j], out = tie(from_chip_back[j], out)
        far_back = lax.ppermute(from_chip_back[j], "seq", other_core)
        states = (turned[j][1], from_chip_back[j], lead[j], rest[j], near_back[j], far_back)
        queries = [q_slots[j, n] for n in range(4)]
        mixed = [local[j, n] for n in range(4)]
        out = finish(where, gain, queries, mixed, states, out, j * 4 * width, width)
    return out


def general_states(k, v, heads_here, nblocks, groups):
    def split(array):
        return array.reshape(nblocks, BLK, heads_here, DH)

    block_sums = jnp.einsum("bthd,bthe->bhde", split(k), split(v), preferred_element_type=F32)
    total = jnp.sum(block_sums, axis=0)
    earlier = jnp.concatenate([jnp.zeros_like(total)[None], jnp.cumsum(block_sums, axis=0)[:-1]])
    gathered = lax.all_gather(total, "seq")
    position = lax.axis_index("seq")
    lower = lax.broadcasted_iota(jnp.int32, (gathered.shape[0], 1, 1, 1), 0) < position
    within = jnp.sum(jnp.where(lower, gathered, 0.0), axis=0)
    group_total = jnp.sum(gathered, axis=0)
    before = jnp.zeros_like(total)
    passing = group_total
    for hop in range(groups - 1):
        received = lax.ppermute(passing, "grp", [(hop, hop + 1)])
        before = before + received
        passing = received + group_total
    return (before + within)[None] + earlier


def general_path(q, k, v, gain, groups, heads_here):
    tokens = q.shape[0]
    nblocks = tokens // BLK
    states = general_states(k, v, heads_here, nblocks, groups).astype(BF16)
    mixed = local_blocks(q, k, v, 1).reshape(nblocks, BLK, heads_here, DH)
    queries = q.reshape(nblocks, BLK, heads_here, DH)
    mixed = mixed + jnp.einsum("bthd,bhde->bthe", queries, states, preferred_element_type=F32)
    meansq = jnp.mean(mixed * mixed, axis=-1, keepdims=True)
    result = mixed * lax.rsqrt(meansq + 1e-05) * gain.reshape(heads_here, DH)
    return result.astype(BF16).reshape(q.shape)


def per_device(groups, shards, query_feat, key_feat, value_feat, norm_gain):
    shape = query_feat.shape
    tokens, width = shape[2:]
    heads_here = width // DH
    q, k, v = (a.reshape(tokens, width) for a in (query_feat, key_feat, value_feat))
    gain = norm_gain.reshape(1, width)
    fits = shards == 4 and groups > 1 and tokens == BLK and heads_here % (4 * CHUNKS) == 0
    path = fast_path if fits else general_path
    return path(q, k, v, gain, groups, heads_here).reshape(shape)


def solution(mesh):
    placed = P("grp", "seq", None, "head")
    return jax.shard_map(
        functools.partial(per_device, mesh.shape["grp"], mesh.shape["seq"]),
        mesh=mesh,
        in_specs=(placed, placed, placed, P("head")),
        out_specs=placed,
        check_vma=False,
    )
```

```python
import functools

import jax
import jax.numpy as jnp
from jax import lax
from jax.experimental import pallas as pl
from jax.experimental.pallas import tpu as pltpu
from jax.sharding import PartitionSpec as P

DH = 128
BLK = 512
TILE = 256
CHUNKS = 2
EARLY = 3
NO_COST = pl.CostEstimate(flops=0, bytes_accessed=0, transcendentals=0)
F32 = jnp.float32
BF16 = jnp.bfloat16
VMEM_LIMIT = 8 * 1024 * 1024


def params():
    return pltpu.CompilerParams(vmem_limit_bytes=VMEM_LIMIT)


def in_hbm(array):
    return pltpu.with_memory_space_constraint(array, pltpu.HBM)


def in_vmem(array):
    return pltpu.with_memory_space_constraint(array, pltpu.VMEM)


def head_cols(i):
    return slice(i * DH, (i + 1) * DH)


def slot_column(slot, width, core, chip):
    half = (slot // 2) ^ core
    quarter = (slot % 2) ^ chip
    return pl.multiple_of((half * 2 + quarter) * width, DH)


class Slots:
    def __init__(self, where_ref, width):
        self.core, self.chip, self.width = where_ref[0], where_ref[1], width

    def column(self, first, slot):
        return pl.multiple_of(first + slot_column(slot, self.width, self.core, self.chip), DH)

    def load(self, first, slot, source, target, sem):
        copy = pltpu.make_async_copy(
            source.at[:, pl.ds(self.column(first, slot), self.width)], target, sem
        )
        copy.start()
        return copy


def specs(*spaces):
    return [pl.BlockSpec(memory_space=s) for s in spaces]


SLOT_ORDER = (3, 2, 0, 1)
KVSUM_OUTS = 6


def kvsum_kernel(width, where_ref, k_hbm, v_hbm, q_hbm, *refs):
    *refs, q_ref, sems = refs
    slots = Slots(where_ref, width)
    outs = [refs[KVSUM_OUTS * j : KVSUM_OUTS * (j + 1)] for j in range(CHUNKS)]
    loads = []
    for slot in SLOT_ORDER:
        for j in range(CHUNKS):
            k_ref, v_ref = outs[j][4:]
            first = 4 * width * j
            loads.append(
                (
                    slot,
                    j,
                    slots.load(first, slot, k_hbm, k_ref.at[slot], sems.at[0, j, slot]),
                    slots.load(first, slot, v_hbm, v_ref.at[slot], sems.at[1, j, slot]),
                )
            )
    q_load = slots.load(0, 0, q_hbm, q_ref, sems.at[2, 0, 0])
    for slot, j, *copies in loads:
        for copy in copies:
            copy.wait()
        lead, rest, own, other, k_ref, v_ref = outs[j]
        for i in range(width // DH):
            c = head_cols(i)
            total = lax.dot_general(
                k_ref[slot, :, c],
                v_ref[slot, :, c],
                (((0,), (0,)), ((), ())),
                preferred_element_type=F32,
            )
            if slot == 3:
                lead[c, :] = total
            else:
                rest[(slot + 1) % 3, c, :] = total
            if slot < 2:
                (own, other)[slot][c, :] = total
    q_load.wait()


def kvsum(where, q, k, v, width):
    tokens = k.shape[0]
    one = pltpu.VMEM((width, DH), F32)
    part = pltpu.VMEM((4, tokens, width), BF16)
    outs = [one, pltpu.VMEM((3, width, DH), F32), one, one, part, part] * CHUNKS
    outs.append(pltpu.VMEM((tokens, width), BF16))
    results = pl.pallas_call(
        functools.partial(kvsum_kernel, width),
        in_specs=specs(pltpu.SMEM, *[pltpu.HBM] * 3),
        out_specs=specs(*[pltpu.VMEM] * len(outs)),
        out_shape=outs,
        scratch_shapes=[pltpu.SemaphoreType.DMA((3, CHUNKS, 4))],
        compiler_params=params(),
        cost_estimate=NO_COST,
        name="kvsum",
    )(where, in_hbm(k), in_hbm(v), in_hbm(q))
    return [results[KVSUM_OUTS * j : KVSUM_OUTS * (j + 1)] for j in range(CHUNKS)], results[-1]


def local_scores(q_ref, k_ref, c):
    rows = lax.broadcasted_iota(jnp.int32, (TILE, TILE), 0)
    cols = lax.broadcasted_iota(jnp.int32, (TILE, TILE), 1)
    causal = rows >= cols
    tiles = []
    for t in range(BLK // TILE):
        scores = lax.dot_general(
            q_ref[t * TILE : (t + 1) * TILE, c],
            k_ref[: (t + 1) * TILE, c],
            (((1,), (1,)), ((), ())),
            preferred_element_type=F32,
        )
        last = jnp.where(causal, scores[:, t * TILE :], 0.0).astype(BF16)
        if t > 0:
            last = jnp.concatenate([scores[:, : t * TILE].astype(BF16), last], axis=1)
        tiles.append(last)
    return tiles


def local_mix(tiles, v_ref, out_ref, c):
    for t, scores in enumerate(tiles):
        out_ref[t * TILE : (t + 1) * TILE, c] = jnp.dot(
            scores, v_ref[: (t + 1) * TILE, c], preferred_element_type=F32
        )


def local_heads(items):
    held = None
    for q_ref, k_ref, v_ref, out_ref, c in items:
        tiles = local_scores(q_ref, k_ref, c)
        if held is not None:
            local_mix(*held)
        held = (tiles, v_ref, out_ref, c)
    local_mix(*held)


def local_kernel(heads, q_ref, k_ref, v_ref, mixed_ref):
    local_heads([(q_ref, k_ref, v_ref, mixed_ref, head_cols(i)) for i in range(heads)])


def local_blocks(q, k, v, heads):
    tokens, width = q.shape
    spec = pl.BlockSpec((BLK, heads * DH), lambda b, s: (b, s))
    return pl.pallas_call(
        functools.partial(local_kernel, heads),
        grid=(tokens // BLK, width // (heads * DH)),
        in_specs=[spec] * 3,
        out_specs=spec,
        out_shape=jax.ShapeDtypeStruct((tokens, width), F32),
        compiler_params=params(),
        name="local_attention",
    )(q, k, v)


def local_slots_kernel(width, places, where_ref, q_hbm, *refs):
    count = len(places)
    if q_hbm is None:
        q_refs, loads = dict(zip(places, refs)), {}
        refs = refs[count:]
    else:
        every = [(j, n) for j in range(CHUNKS) for n in range(4)]
        *refs, sems = refs
        q_refs = dict(zip(every, [refs[0], *refs[-len(every) + 1 :]]))
        refs = refs[1:]
        slots = Slots(where_ref, width)
        loads = {
            (j, n): slots.load(4 * width * j, n, q_hbm, q_refs[j, n], sems.at[j, n])
            for j, n in every[1:]
        }
    k_refs, v_refs, out_refs = refs[:CHUNKS], refs[CHUNKS : 2 * CHUNKS], refs[2 * CHUNKS :]

    def items():
        for place, out_ref in zip(places, out_refs):
            j, n = place
            if place in loads:
                loads.pop(place).wait()
            for i in range(width // DH):
                yield q_refs[place], k_refs[j].at[n], v_refs[j].at[n], out_ref, head_cols(i)

    local_heads(items())
    for copy in loads.values():
        copy.wait()


def local_slots(where, q, q_lead, q_slots, k_parts, v_parts, width, places):
    tokens = k_parts[0].shape[1]
    first = q_lead is not None
    every = 4 * CHUNKS
    kernel = functools.partial(local_slots_kernel, width, places)
    if not first:
        kernel = lambda where_ref, *refs: local_slots_kernel(width, places, where_ref, None, *refs)
    queries = [q_lead] if first else [q_slots[p] for p in places]
    outs = [pltpu.VMEM((tokens, width), F32)] * len(places)
    outs += [pltpu.VMEM((tokens, width), BF16)] * ((every - 1) * first)
    results = pl.pallas_call(
        kernel,
        in_specs=specs(
            pltpu.SMEM, *[pltpu.HBM] * first, *[pltpu.VMEM] * (len(queries) + 2 * CHUNKS)
        ),
        out_specs=specs(*[pltpu.VMEM] * len(outs)),
        out_shape=outs,
        scratch_shapes=[pltpu.SemaphoreType.DMA((CHUNKS, 4))] * first,
        compiler_params=params(),
        cost_estimate=NO_COST,
        name="local_attention",
    )(where, *([in_hbm(q)] if first else []), *[in_vmem(a) for a in (*queries, *k_parts, *v_parts)])
    return results[: len(places)], results[len(places) :]


def finish_kernel(first, width, where_ref, gain_ref, *refs):
    q_refs, mixed_refs = refs[:4], refs[4:8]
    own_near, own_far, lead_ref, rest_ref, far_near, far_far = refs[8:14]
    out_hbm, out_ref, sems = refs[-3:]
    slots = Slots(where_ref, width)
    second = slots.core.astype(F32)
    states = (own_near, own_far, far_near, far_far)
    from_core = (rest_ref.at[0], lead_ref, rest_ref.at[1], rest_ref.at[2])
    stores = []
    for n in range(4):
        column = slots.column(first, n)
        for i in range(width // DH):
            c = head_cols(i)
            state = states[n][c, :] + second * from_core[n][c, :]
            mixed = mixed_refs[n][:, c] + jnp.dot(
                q_refs[n][:, c], state.astype(BF16), preferred_element_type=F32
            )
            meansq = jnp.mean(mixed * mixed, axis=-1, keepdims=True)
            gain = gain_ref[:, pl.ds(pl.multiple_of(column + i * DH, DH), DH)]
            out_ref[n, :, c] = (mixed * lax.rsqrt(meansq + 1e-05) * gain).astype(BF16)
        store = pltpu.make_async_copy(out_ref.at[n], out_hbm.at[:, pl.ds(column, width)], sems.at[n])
        store.start()
        stores.append(store)
    for store in stores:
        store.wait()


def finish(where, gain, queries, mixed, states, out, first, width):
    tokens = queries[0].shape[0]
    earlier = [] if out is None else [out]
    operands = [where, gain, *[in_vmem(a) for a in (*queries, *mixed)], *states]
    return pl.pallas_call(
        functools.partial(finish_kernel, first, width),
        in_specs=specs(pltpu.SMEM, *[pltpu.VMEM] * (len(operands) - 1), *[pltpu.HBM] * len(earlier)),
        out_specs=specs(pltpu.HBM)[0],
        out_shape=jax.ShapeDtypeStruct((tokens, gain.shape[1]), BF16),
        scratch_shapes=[pltpu.VMEM((4, tokens, width), BF16), pltpu.SemaphoreType.DMA((4,))],
        input_output_aliases={len(operands): 0} if earlier else {},
        compiler_params=params(),
        cost_estimate=NO_COST,
        name="finish",
    )(*operands, *earlier)


def combine(compute, count, where, *operands):
    shape = operands[0].shape

    def kernel(where_ref, *refs):
        ins, outs = refs[: len(operands)], refs[len(operands) :]
        core, chip = where_ref[0].astype(F32), where_ref[1].astype(F32)
        results = compute(core, chip, *[r[...] for r in ins])
        for ref, value in zip(outs, results):
            ref[...] = value

    return pl.pallas_call(
        kernel,
        in_specs=specs(pltpu.SMEM, *[pltpu.VMEM] * len(operands)),
        out_specs=specs(*[pltpu.VMEM] * count),
        out_shape=[jax.ShapeDtypeStruct(shape, F32)] * count,
        compiler_params=params(),
        cost_estimate=NO_COST,
        name="combine",
    )(where, *operands)


def send(name, array, axis, pairs):
    with jax.named_scope(name):
        return lax.ppermute(array, axis, pairs)


def tie(*values):
    return lax.optimization_barrier(values)


def fast_path(q, k, v, gain, groups, heads_here):
    chunks = range(CHUNKS)
    width = heads_here // (4 * CHUNKS) * DH
    position = lax.axis_index("seq")
    core, chip = position % 2, position // 2
    where = jnp.stack([core, chip]).astype(jnp.int32)
    other_core = [(0, 1), (1, 0), (2, 3), (3, 2)]
    other_chip = [(0, 2), (2, 0), (1, 3), (3, 1)]

    sums, q_lead = kvsum(where, q, k, v, width)
    lead = [send(f"lead{j}", s[0], "seq", other_core) for j, s in enumerate(sums)]
    there = [s[3] + r for s, r in zip(sums, lead)]
    rest = []
    for j, s in enumerate(sums):
        there[0], held = tie(there[0], s[1])
        rest.append(send(f"rest{j}", held, "seq", other_core))
    k_parts, v_parts = [s[4] for s in sums], [s[5] for s in sums]
    every = [(j, n) for j in chunks for n in range(4)]
    local, q_slots = [], None
    for j in chunks[:-1]:
        there[j], held = tie(there[j], where)
        places = every[len(local) : len(local) + EARLY]
        if j == 0:
            part, q_slots = local_slots(held, q, q_lead, None, k_parts, v_parts, width, places)
            q_slots = dict(zip(every, [q_lead, *q_slots]))
        else:
            part, _ = local_slots(held, None, None, q_slots, k_parts, v_parts, width, places)
        there[j + 1], part = tie(there[j + 1], part)
        local += part
    from_chip = [send(f"chip{j}", t, "seq", other_chip) for j, t in enumerate(there)]
    here = [s[2] + r[0] for s, r in zip(sums, rest)]
    group_total = [h + r for h, r in zip(here, from_chip)]

    arrived = [[] for _ in chunks]
    passing = group_total
    for hop in range(groups - 1):
        if hop == min(1, groups - 2):
            passing[-1], held = tie(passing[-1], where)
            late, _ = local_slots(held, None, None, q_slots, k_parts, v_parts, width, every[len(local) :])
        received = [send(f"hop{hop}_{j}", p, "grp", [(hop, hop + 1)]) for j, p in enumerate(passing)]
        if hop == min(1, groups - 2):
            received[0], late = tie(received[0], late)
        for j in chunks:
            arrived[j].append(received[j])
        passing = [r + g for r, g in zip(received, group_total)]

    local = dict(zip(every, [*local, *late]))

    def turn(core, chip, here, from_chip, *arrived):
        before = sum(arrived[1:], arrived[0])
        return before + (1.0 - chip) * here, before + chip * from_chip

    turned = [combine(turn, 2, where, here[j], from_chip[j], *arrived[j]) for j in chunks]
    from_chip_back = [send(f"chipback{j}", t[0], "seq", other_chip) for j, t in enumerate(turned)]
    near_back = [send(f"near{j}", t[1], "seq", other_core) for j, t in enumerate(turned)]
    out = None
    for j in chunks:
        far_back = send(f"far{j}", from_chip_back[j], "seq", other_core)
        states = (turned[j][1], from_chip_back[j], lead[j], rest[j], near_back[j], far_back)
        queries = [q_slots[j, n] for n in range(4)]
        mixed = [local[j, n] for n in range(4)]
        out = finish(where, gain, queries, mixed, states, out, j * 4 * width, width)
    return out


def general_states(k, v, heads_here, nblocks, groups):
    def split(array):
        return array.reshape(nblocks, BLK, heads_here, DH)

    block_sums = jnp.einsum("bthd,bthe->bhde", split(k), split(v), preferred_element_type=F32)
    total = jnp.sum(block_sums, axis=0)
    earlier = jnp.concatenate([jnp.zeros_like(total)[None], jnp.cumsum(block_sums, axis=0)[:-1]])
    gathered = lax.all_gather(total, "seq")
    position = lax.axis_index("seq")
    lower = lax.broadcasted_iota(jnp.int32, (gathered.shape[0], 1, 1, 1), 0) < position
    within = jnp.sum(jnp.where(lower, gathered, 0.0), axis=0)
    group_total = jnp.sum(gathered, axis=0)
    before = jnp.zeros_like(total)
    passing = group_total
    for hop in range(groups - 1):
        received = lax.ppermute(passing, "grp", [(hop, hop + 1)])
        before = before + received
        passing = received + group_total
    return (before + within)[None] + earlier


def general_path(q, k, v, gain, groups, heads_here):
    tokens = q.shape[0]
    nblocks = tokens // BLK
    states = general_states(k, v, heads_here, nblocks, groups).astype(BF16)
    mixed = local_blocks(q, k, v, 1).reshape(nblocks, BLK, heads_here, DH)
    queries = q.reshape(nblocks, BLK, heads_here, DH)
    mixed = mixed + jnp.einsum("bthd,bhde->bthe", queries, states, preferred_element_type=F32)
    meansq = jnp.mean(mixed * mixed, axis=-1, keepdims=True)
    result = mixed * lax.rsqrt(meansq + 1e-05) * gain.reshape(heads_here, DH)
    return result.astype(BF16).reshape(q.shape)


def per_device(groups, shards, query_feat, key_feat, value_feat, norm_gain):
    shape = query_feat.shape
    tokens, width = shape[2:]
    heads_here = width // DH
    q, k, v = (a.reshape(tokens, width) for a in (query_feat, key_feat, value_feat))
    gain = norm_gain.reshape(1, width)
    fits = shards == 4 and groups > 1 and tokens == BLK and heads_here % (4 * CHUNKS) == 0
    path = fast_path if fits else general_path
    return path(q, k, v, gain, groups, heads_here).reshape(shape)


def solution(mesh):
    placed = P("grp", "seq", None, "head")
    return jax.shard_map(
        functools.partial(per_device, mesh.shape["grp"], mesh.shape["seq"]),
        mesh=mesh,
        in_specs=(placed, placed, placed, P("head")),
        out_specs=placed,
        check_vma=False,
    )
```

```python
import functools

import jax
import jax.numpy as jnp
from jax import lax
from jax.experimental import pallas as pl
from jax.experimental.pallas import tpu as pltpu
from jax.sharding import PartitionSpec as P

DH = 128
BLK = 512
TILE = 256
CHUNKS = 2
EARLY = 2
NO_COST = pl.CostEstimate(flops=0, bytes_accessed=0, transcendentals=0)
F32 = jnp.float32
BF16 = jnp.bfloat16
VMEM_LIMIT = 8 * 1024 * 1024


def params():
    return pltpu.CompilerParams(vmem_limit_bytes=VMEM_LIMIT)


def in_hbm(array):
    return pltpu.with_memory_space_constraint(array, pltpu.HBM)


def in_vmem(array):
    return pltpu.with_memory_space_constraint(array, pltpu.VMEM)


def head_cols(i):
    return slice(i * DH, (i + 1) * DH)


def slot_column(slot, width, core, chip):
    half = (slot // 2) ^ core
    quarter = (slot % 2) ^ chip
    return pl.multiple_of((half * 2 + quarter) * width, DH)


def place():
    position = lax.axis_index("seq")
    return position & 1, position >> 1


class Slots:
    def __init__(self, width):
        (self.core, self.chip), self.width = place(), width

    def column(self, first, slot):
        return pl.multiple_of(first + slot_column(slot, self.width, self.core, self.chip), DH)

    def load(self, first, slot, source, target, sem):
        copy = pltpu.make_async_copy(
            source.at[:, pl.ds(self.column(first, slot), self.width)], target, sem
        )
        copy.start()
        return copy


def specs(*spaces):
    return [pl.BlockSpec(memory_space=s) for s in spaces]


SLOT_ORDER = (3, 2, 0, 1)
KVSUM_OUTS = 4


def kvsum_kernel(width, k_hbm, v_hbm, q_hbm, *refs):
    *refs, lead, rest, q_ref, sems = refs
    slots = Slots(width)
    outs = [refs[KVSUM_OUTS * j : KVSUM_OUTS * (j + 1)] for j in range(CHUNKS)]
    loads = []
    for slot in SLOT_ORDER:
        for j in range(CHUNKS):
            k_ref, v_ref = outs[j][2:]
            first = 4 * width * j
            loads.append(
                (
                    slot,
                    j,
                    slots.load(first, slot, k_hbm, k_ref.at[slot], sems.at[0, j, slot]),
                    slots.load(first, slot, v_hbm, v_ref.at[slot], sems.at[1, j, slot]),
                )
            )
    q_load = slots.load(0, 0, q_hbm, q_ref, sems.at[2, 0, 0])
    for slot, j, *copies in loads:
        for copy in copies:
            copy.wait()
        own, other, k_ref, v_ref = outs[j]
        for i in range(width // DH):
            c = head_cols(i)
            total = lax.dot_general(
                k_ref[slot, :, c],
                v_ref[slot, :, c],
                (((0,), (0,)), ((), ())),
                preferred_element_type=F32,
            )
            if slot == 3:
                lead[j, c, :] = total
            else:
                rest[j, (slot + 1) % 3, c, :] = total
            if slot < 2:
                (own, other)[slot][c, :] = total
    q_load.wait()


def kvsum(q, k, v, width):
    tokens = k.shape[0]
    one = pltpu.VMEM((width, DH), F32)
    part = pltpu.VMEM((4, tokens, width), BF16)
    outs = [one, one, part, part] * CHUNKS
    outs += [pltpu.VMEM((CHUNKS, width, DH), F32), pltpu.VMEM((CHUNKS, 3, width, DH), F32)]
    outs.append(pltpu.VMEM((tokens, width), BF16))
    results = pl.pallas_call(
        functools.partial(kvsum_kernel, width),
        in_specs=specs(*[pltpu.HBM] * 3),
        out_specs=specs(*[pltpu.VMEM] * len(outs)),
        out_shape=outs,
        scratch_shapes=[pltpu.SemaphoreType.DMA((3, CHUNKS, 4))],
        compiler_params=params(),
        cost_estimate=NO_COST,
        name="kvsum",
    )(in_hbm(k), in_hbm(v), in_hbm(q))
    return [results[KVSUM_OUTS * j : KVSUM_OUTS * (j + 1)] for j in range(CHUNKS)], results[-3:]


def local_scores(q_ref, k_ref, c):
    rows = lax.broadcasted_iota(jnp.int32, (TILE, TILE), 0)
    cols = lax.broadcasted_iota(jnp.int32, (TILE, TILE), 1)
    causal = rows >= cols
    tiles = []
    for t in range(BLK // TILE):
        scores = lax.dot_general(
            q_ref[t * TILE : (t + 1) * TILE, c],
            k_ref[: (t + 1) * TILE, c],
            (((1,), (1,)), ((), ())),
            preferred_element_type=F32,
        )
        last = jnp.where(causal, scores[:, t * TILE :], 0.0).astype(BF16)
        if t > 0:
            last = jnp.concatenate([scores[:, : t * TILE].astype(BF16), last], axis=1)
        tiles.append(last)
    return tiles


def local_mix(tiles, v_ref, out_ref, c):
    for t, scores in enumerate(tiles):
        out_ref[t * TILE : (t + 1) * TILE, c] = jnp.dot(
            scores, v_ref[: (t + 1) * TILE, c], preferred_element_type=F32
        )


def local_heads(items):
    held = None
    for q_ref, k_ref, v_ref, out_ref, c in items:
        tiles = local_scores(q_ref, k_ref, c)
        if held is not None:
            local_mix(*held)
        held = (tiles, v_ref, out_ref, c)
    local_mix(*held)


def local_kernel(heads, q_ref, k_ref, v_ref, mixed_ref):
    local_heads([(q_ref, k_ref, v_ref, mixed_ref, head_cols(i)) for i in range(heads)])


def local_blocks(q, k, v, heads):
    tokens, width = q.shape
    spec = pl.BlockSpec((BLK, heads * DH), lambda b, s: (b, s))
    return pl.pallas_call(
        functools.partial(local_kernel, heads),
        grid=(tokens // BLK, width // (heads * DH)),
        in_specs=[spec] * 3,
        out_specs=spec,
        out_shape=jax.ShapeDtypeStruct((tokens, width), F32),
        compiler_params=params(),
        name="local_attention",
    )(q, k, v)


def local_slots_kernel(width, places, q_hbm, *refs):
    count = len(places)
    if q_hbm is None:
        q_refs, loads = dict(zip(places, refs)), {}
        refs = refs[count:]
    else:
        every = [(j, n) for j in range(CHUNKS) for n in range(4)]
        *refs, sems = refs
        q_refs = dict(zip(every, [refs[0], *refs[-len(every) + 1 :]]))
        refs = refs[1:]
        slots = Slots(width)
        loads = {
            (j, n): slots.load(4 * width * j, n, q_hbm, q_refs[j, n], sems.at[j, n])
            for j, n in every[1:]
        }
    k_refs, v_refs, out_refs = refs[:CHUNKS], refs[CHUNKS : 2 * CHUNKS], refs[2 * CHUNKS :]

    def items():
        for place, out_ref in zip(places, out_refs):
            j, n = place
            if place in loads:
                loads.pop(place).wait()
            for i in range(width // DH):
                yield q_refs[place], k_refs[j].at[n], v_refs[j].at[n], out_ref, head_cols(i)

    local_heads(items())
    for copy in loads.values():
        copy.wait()


def local_slots(q, q_lead, q_slots, k_parts, v_parts, width, places):
    tokens = k_parts[0].shape[1]
    first = q_lead is not None
    every = 4 * CHUNKS
    kernel = functools.partial(local_slots_kernel, width, places)
    if not first:
        kernel = lambda *refs: local_slots_kernel(width, places, None, *refs)
    queries = [q_lead] if first else [q_slots[p] for p in places]
    outs = [pltpu.VMEM((tokens, width), F32)] * len(places)
    outs += [pltpu.VMEM((tokens, width), BF16)] * ((every - 1) * first)
    results = pl.pallas_call(
        kernel,
        in_specs=specs(*[pltpu.HBM] * first, *[pltpu.VMEM] * (len(queries) + 2 * CHUNKS)),
        out_specs=specs(*[pltpu.VMEM] * len(outs)),
        out_shape=outs,
        scratch_shapes=[pltpu.SemaphoreType.DMA((CHUNKS, 4))] * first,
        compiler_params=params(),
        cost_estimate=NO_COST,
        name="local_attention",
    )(*([in_hbm(q)] if first else []), *[in_vmem(a) for a in (*queries, *k_parts, *v_parts)])
    return results[: len(places)], results[len(places) :]


def finish_kernel(places, width, gain_ref, *refs):
    out_hbm, out_ref, sems = refs[-3:]
    slots = Slots(width)
    second = slots.core.astype(F32)
    stores = []
    for m, (j, n) in enumerate(places):
        q_ref, mixed_ref, state_ref, from_core = refs[4 * m : 4 * m + 4]
        column = slots.column(4 * width * j, n)
        for i in range(width // DH):
            c = head_cols(i)
            other = from_core[j, c, :] if n == 1 else from_core[j, max(n - 1, 0), c, :]
            state = state_ref[c, :] + second * other
            mixed = mixed_ref[:, c] + jnp.dot(
                q_ref[:, c], state.astype(BF16), preferred_element_type=F32
            )
            meansq = jnp.mean(mixed * mixed, axis=-1, keepdims=True)
            gain = gain_ref[:, pl.ds(pl.multiple_of(column + i * DH, DH), DH)]
            out_ref[m, :, c] = (mixed * lax.rsqrt(meansq + 1e-05) * gain).astype(BF16)
        store = pltpu.make_async_copy(out_ref.at[m], out_hbm.at[:, pl.ds(column, width)], sems.at[m])
        store.start()
        stores.append(store)
    for store in stores:
        store.wait()


def finish(gain, slots, out, width):
    places = list(slots)
    tokens = slots[places[0]][0].shape[0]
    earlier = [] if out is None else [out]
    operands = [gain]
    for q, mixed, state, from_core in slots.values():
        operands += [in_vmem(q), in_vmem(mixed), state, from_core]
    return pl.pallas_call(
        functools.partial(finish_kernel, places, width),
        in_specs=specs(*[pltpu.VMEM] * len(operands), *[pltpu.HBM] * len(earlier)),
        out_specs=specs(pltpu.HBM)[0],
        out_shape=jax.ShapeDtypeStruct((tokens, gain.shape[1]), BF16),
        scratch_shapes=[
            pltpu.VMEM((len(places), tokens, width), BF16),
            pltpu.SemaphoreType.DMA((len(places),)),
        ],
        input_output_aliases={len(operands): 0} if earlier else {},
        compiler_params=params(),
        cost_estimate=NO_COST,
        name="finish",
    )(*operands, *earlier)


def combine(compute, count, *operands):
    shape = operands[0].shape

    def kernel(*refs):
        ins, outs = refs[: len(operands)], refs[len(operands) :]
        core, chip = (a.astype(F32) for a in place())
        results = compute(core, chip, *[r[...] for r in ins])
        for ref, value in zip(outs, results):
            ref[...] = value

    results = pl.pallas_call(
        kernel,
        in_specs=specs(*[pltpu.VMEM] * len(operands)),
        out_specs=specs(*[pltpu.VMEM] * count),
        out_shape=[jax.ShapeDtypeStruct(shape, F32)] * count,
        compiler_params=params(),
        cost_estimate=NO_COST,
        name="combine",
    )(*operands)
    return list(results)


def send(name, array, axis, pairs):
    with jax.named_scope(name):
        return lax.ppermute(array, axis, pairs)


def add_to(core, chip, *arrays):
    *arrays, parts = arrays
    return [a + (parts[j] if parts.ndim == 3 else parts[j, 0]) for j, a in enumerate(arrays)]


def tie(*values):
    return lax.optimization_barrier(values)


def fast_path(q, k, v, gain, groups, heads_here):
    chunks = range(CHUNKS)
    width = heads_here // (4 * CHUNKS) * DH
    position = lax.axis_index("seq")
    core, chip = position % 2, position // 2
    where = jnp.stack([core, chip]).astype(jnp.int32)
    other_core = [(0, 1), (1, 0), (2, 3), (3, 2)]
    other_chip = [(0, 2), (2, 0), (1, 3), (3, 1)]

    sums, (lead, rest, q_lead) = kvsum(q, k, v, width)
    lead = send("lead", lead, "seq", other_core)
    there = combine(add_to, CHUNKS, *[s[1] for s in sums], lead)
    there[0], rest = tie(there[0], rest)
    rest = send("rest", rest, "seq", other_core)
    k_parts, v_parts = [s[2] for s in sums], [s[3] for s in sums]
    every = [(j, n) for j in chunks for n in range(4)]
    local, q_slots = [], None
    for j in chunks[:-1]:
        there[j], k_parts[0] = tie(there[j], k_parts[0])
        places = every[len(local) : len(local) + EARLY]
        if j == 0:
            part, q_slots = local_slots(q, q_lead, None, k_parts, v_parts, width, places)
            q_slots = dict(zip(every, [q_lead, *q_slots]))
        else:
            part, _ = local_slots(None, None, q_slots, k_parts, v_parts, width, places)
        there[j + 1], part = tie(there[j + 1], part)
        local += part
    from_chip = [send(f"chip{j}", t, "seq", other_chip) for j, t in enumerate(there)]
    here = combine(add_to, CHUNKS, *[s[0] for s in sums], rest)
    group_total = [h + r for h, r in zip(here, from_chip)]

    arrived = [[] for _ in chunks]
    passing = group_total
    for hop in range(groups - 1):
        if hop == min(1, groups - 2):
            passing[-1], k_parts[0] = tie(passing[-1], k_parts[0])
            late, _ = local_slots(None, None, q_slots, k_parts, v_parts, width, every[len(local) :])
        received = [send(f"hop{hop}_{j}", p, "grp", [(hop, hop + 1)]) for j, p in enumerate(passing)]
        if hop == min(1, groups - 2):
            received[0], late = tie(received[0], late)
        for j in chunks:
            arrived[j].append(received[j])
        passing = [r + g for r, g in zip(received, group_total)]

    local = dict(zip(every, [*local, *late]))

    def turn(core, chip, here, from_chip, *arrived):
        before = sum(arrived[1:], arrived[0])
        return before + (1.0 - chip) * here, before + chip * from_chip

    turned = [combine(turn, 2, here[j], from_chip[j], *arrived[j]) for j in chunks]
    from_chip_back = [send(f"chipback{j}", t[0], "seq", other_chip) for j, t in enumerate(turned)]
    near_back = [send(f"near{j}", t[1], "seq", other_core) for j, t in enumerate(turned)]
    def near_slots(j):
        return {
            (j, 0): (q_slots[j, 0], local[j, 0], turned[j][1], rest),
            (j, 1): (q_slots[j, 1], local[j, 1], from_chip_back[j], lead),
        }

    def far_slots(j):
        far_back = send(f"far{j}", from_chip_back[j], "seq", other_core)
        return {
            (j, 2): (q_slots[j, 2], local[j, 2], near_back[j], rest),
            (j, 3): (q_slots[j, 3], local[j, 3], far_back, rest),
        }

    out, slots = None, {}
    for j in chunks:
        out = finish(gain, {**slots, **near_slots(j)}, out, width)
        slots = far_slots(j)
        if j + 1 < CHUNKS:
            from_chip_back[j + 1], out = tie(from_chip_back[j + 1], out)
    return finish(gain, slots, out, width)


def general_states(k, v, heads_here, nblocks, groups):
    def split(array):
        return array.reshape(nblocks, BLK, heads_here, DH)

    block_sums = jnp.einsum("bthd,bthe->bhde", split(k), split(v), preferred_element_type=F32)
    total = jnp.sum(block_sums, axis=0)
    earlier = jnp.concatenate([jnp.zeros_like(total)[None], jnp.cumsum(block_sums, axis=0)[:-1]])
    gathered = lax.all_gather(total, "seq")
    position = lax.axis_index("seq")
    lower = lax.broadcasted_iota(jnp.int32, (gathered.shape[0], 1, 1, 1), 0) < position
    within = jnp.sum(jnp.where(lower, gathered, 0.0), axis=0)
    group_total = jnp.sum(gathered, axis=0)
    before = jnp.zeros_like(total)
    passing = group_total
    for hop in range(groups - 1):
        received = lax.ppermute(passing, "grp", [(hop, hop + 1)])
        before = before + received
        passing = received + group_total
    return (before + within)[None] + earlier


def general_path(q, k, v, gain, groups, heads_here):
    tokens = q.shape[0]
    nblocks = tokens // BLK
    states = general_states(k, v, heads_here, nblocks, groups).astype(BF16)
    mixed = local_blocks(q, k, v, 1).reshape(nblocks, BLK, heads_here, DH)
    queries = q.reshape(nblocks, BLK, heads_here, DH)
    mixed = mixed + jnp.einsum("bthd,bhde->bthe", queries, states, preferred_element_type=F32)
    meansq = jnp.mean(mixed * mixed, axis=-1, keepdims=True)
    result = mixed * lax.rsqrt(meansq + 1e-05) * gain.reshape(heads_here, DH)
    return result.astype(BF16).reshape(q.shape)


def per_device(groups, shards, query_feat, key_feat, value_feat, norm_gain):
    shape = query_feat.shape
    tokens, width = shape[2:]
    heads_here = width // DH
    q, k, v = (a.reshape(tokens, width) for a in (query_feat, key_feat, value_feat))
    gain = norm_gain.reshape(1, width)
    fits = shards == 4 and groups > 1 and tokens == BLK and heads_here % (4 * CHUNKS) == 0
    path = fast_path if fits else general_path
    return path(q, k, v, gain, groups, heads_here).reshape(shape)


def solution(mesh):
    placed = P("grp", "seq", None, "head")
    return jax.shard_map(
        functools.partial(per_device, mesh.shape["grp"], mesh.shape["seq"]),
        mesh=mesh,
        in_specs=(placed, placed, placed, P("head")),
        out_specs=placed,
        check_vma=False,
    )
```

```python
import functools

import jax
import jax.numpy as jnp
from jax import lax
from jax.experimental import pallas as pl
from jax.experimental.pallas import tpu as pltpu
from jax.sharding import PartitionSpec as P

DH = 128
BLK = 512
TILE = 256
CHUNKS = 2
EARLY = 4
NO_COST = pl.CostEstimate(flops=0, bytes_accessed=0, transcendentals=0)
F32 = jnp.float32
BF16 = jnp.bfloat16
VMEM_LIMIT = 8 * 1024 * 1024


def params():
    return pltpu.CompilerParams(vmem_limit_bytes=VMEM_LIMIT)


def in_hbm(array):
    return pltpu.with_memory_space_constraint(array, pltpu.HBM)


def in_vmem(array):
    return pltpu.with_memory_space_constraint(array, pltpu.VMEM)


def head_cols(i):
    return slice(i * DH, (i + 1) * DH)


def slot_column(slot, width, core, chip):
    half = (slot // 2) ^ core
    quarter = (slot % 2) ^ chip
    return pl.multiple_of((half * 2 + quarter) * width, DH)


def place():
    position = lax.axis_index("seq")
    return position & 1, position >> 1


class Slots:
    def __init__(self, width):
        (self.core, self.chip), self.width = place(), width

    def column(self, first, slot):
        return pl.multiple_of(first + slot_column(slot, self.width, self.core, self.chip), DH)

    def load(self, first, slot, source, target, sem):
        copy = pltpu.make_async_copy(
            source.at[:, pl.ds(self.column(first, slot), self.width)], target, sem
        )
        copy.start()
        return copy


def specs(*spaces):
    return [pl.BlockSpec(memory_space=s) for s in spaces]


SLOT_ORDER = (3, 2, 0, 1)
KVSUM_OUTS = 4


def kvsum_kernel(width, k_hbm, v_hbm, q_hbm, *refs):
    *refs, lead, rest, q_ref, sems = refs
    slots = Slots(width)
    outs = [refs[KVSUM_OUTS * j : KVSUM_OUTS * (j + 1)] for j in range(CHUNKS)]
    loads = []
    for slot in SLOT_ORDER:
        for j in range(CHUNKS):
            k_ref, v_ref = outs[j][2:]
            first = 4 * width * j
            loads.append(
                (
                    slot,
                    j,
                    slots.load(first, slot, k_hbm, k_ref.at[slot], sems.at[0, j, slot]),
                    slots.load(first, slot, v_hbm, v_ref.at[slot], sems.at[1, j, slot]),
                )
            )
    q_load = slots.load(0, 0, q_hbm, q_ref, sems.at[2, 0, 0])
    for slot, j, *copies in loads:
        for copy in copies:
            copy.wait()
        own, other, k_ref, v_ref = outs[j]
        for i in range(width // DH):
            c = head_cols(i)
            total = lax.dot_general(
                k_ref[slot, :, c],
                v_ref[slot, :, c],
                (((0,), (0,)), ((), ())),
                preferred_element_type=F32,
            )
            if slot == 3:
                lead[j, c, :] = total
            else:
                rest[j, (slot + 1) % 3, c, :] = total
            if slot < 2:
                (own, other)[slot][c, :] = total
    q_load.wait()


def kvsum(q, k, v, width):
    tokens = k.shape[0]
    one = pltpu.VMEM((width, DH), F32)
    part = pltpu.VMEM((4, tokens, width), BF16)
    outs = [one, one, part, part] * CHUNKS
    outs += [pltpu.VMEM((CHUNKS, width, DH), F32), pltpu.VMEM((CHUNKS, 3, width, DH), F32)]
    outs.append(pltpu.VMEM((tokens, width), BF16))
    results = pl.pallas_call(
        functools.partial(kvsum_kernel, width),
        in_specs=specs(*[pltpu.HBM] * 3),
        out_specs=specs(*[pltpu.VMEM] * len(outs)),
        out_shape=outs,
        scratch_shapes=[pltpu.SemaphoreType.DMA((3, CHUNKS, 4))],
        compiler_params=params(),
        cost_estimate=NO_COST,
        name="kvsum",
    )(in_hbm(k), in_hbm(v), in_hbm(q))
    return [results[KVSUM_OUTS * j : KVSUM_OUTS * (j + 1)] for j in range(CHUNKS)], results[-3:]


def local_scores(q_ref, k_ref, c):
    rows = lax.broadcasted_iota(jnp.int32, (TILE, TILE), 0)
    cols = lax.broadcasted_iota(jnp.int32, (TILE, TILE), 1)
    causal = rows >= cols
    tiles = []
    for t in range(BLK // TILE):
        scores = lax.dot_general(
            q_ref[t * TILE : (t + 1) * TILE, c],
            k_ref[: (t + 1) * TILE, c],
            (((1,), (1,)), ((), ())),
            preferred_element_type=F32,
        )
        last = jnp.where(causal, scores[:, t * TILE :], 0.0).astype(BF16)
        if t > 0:
            last = jnp.concatenate([scores[:, : t * TILE].astype(BF16), last], axis=1)
        tiles.append(last)
    return tiles


def local_mix(tiles, v_ref, out_ref, c):
    for t, scores in enumerate(tiles):
        out_ref[t * TILE : (t + 1) * TILE, c] = jnp.dot(
            scores, v_ref[: (t + 1) * TILE, c], preferred_element_type=F32
        )


def local_heads(items):
    held = None
    for q_ref, k_ref, v_ref, out_ref, c in items:
        tiles = local_scores(q_ref, k_ref, c)
        if held is not None:
            local_mix(*held)
        held = (tiles, v_ref, out_ref, c)
    local_mix(*held)


def local_kernel(heads, q_ref, k_ref, v_ref, mixed_ref):
    local_heads([(q_ref, k_ref, v_ref, mixed_ref, head_cols(i)) for i in range(heads)])


def local_blocks(q, k, v, heads):
    tokens, width = q.shape
    spec = pl.BlockSpec((BLK, heads * DH), lambda b, s: (b, s))
    return pl.pallas_call(
        functools.partial(local_kernel, heads),
        grid=(tokens // BLK, width // (heads * DH)),
        in_specs=[spec] * 3,
        out_specs=spec,
        out_shape=jax.ShapeDtypeStruct((tokens, width), F32),
        compiler_params=params(),
        name="local_attention",
    )(q, k, v)


def local_slots_kernel(width, places, q_hbm, *refs):
    count = len(places)
    if q_hbm is None:
        q_refs, loads = dict(zip(places, refs)), {}
        refs = refs[count:]
    else:
        every = [(j, n) for j in range(CHUNKS) for n in range(4)]
        *refs, sems = refs
        q_refs = dict(zip(every, [refs[0], *refs[-len(every) + 1 :]]))
        refs = refs[1:]
        slots = Slots(width)
        loads = {
            (j, n): slots.load(4 * width * j, n, q_hbm, q_refs[j, n], sems.at[j, n])
            for j, n in every[1:]
        }
    k_refs, v_refs, out_refs = refs[:CHUNKS], refs[CHUNKS : 2 * CHUNKS], refs[2 * CHUNKS :]

    def items():
        for place, out_ref in zip(places, out_refs):
            j, n = place
            if place in loads:
                loads.pop(place).wait()
            for i in range(width // DH):
                yield q_refs[place], k_refs[j].at[n], v_refs[j].at[n], out_ref, head_cols(i)

    local_heads(items())
    for copy in loads.values():
        copy.wait()


def local_slots(q, q_lead, q_slots, k_parts, v_parts, width, places):
    tokens = k_parts[0].shape[1]
    first = q_lead is not None
    every = 4 * CHUNKS
    kernel = functools.partial(local_slots_kernel, width, places)
    if not first:
        kernel = lambda *refs: local_slots_kernel(width, places, None, *refs)
    queries = [q_lead] if first else [q_slots[p] for p in places]
    outs = [pltpu.VMEM((tokens, width), F32)] * len(places)
    outs += [pltpu.VMEM((tokens, width), BF16)] * ((every - 1) * first)
    results = pl.pallas_call(
        kernel,
        in_specs=specs(*[pltpu.HBM] * first, *[pltpu.VMEM] * (len(queries) + 2 * CHUNKS)),
        out_specs=specs(*[pltpu.VMEM] * len(outs)),
        out_shape=outs,
        scratch_shapes=[pltpu.SemaphoreType.DMA((CHUNKS, 4))] * first,
        compiler_params=params(),
        cost_estimate=NO_COST,
        name="local_attention",
    )(*([in_hbm(q)] if first else []), *[in_vmem(a) for a in (*queries, *k_parts, *v_parts)])
    return results[: len(places)], results[len(places) :]


def finish_kernel(places, width, gain_ref, *refs):
    out_hbm, out_ref, sems = refs[-3:]
    slots = Slots(width)
    second = slots.core.astype(F32)
    stores = []
    for m, (j, n) in enumerate(places):
        q_ref, mixed_ref, state_ref, from_core = refs[4 * m : 4 * m + 4]
        column = slots.column(4 * width * j, n)
        for i in range(width // DH):
            c = head_cols(i)
            other = from_core[j, c, :] if n == 1 else from_core[j, max(n - 1, 0), c, :]
            state = state_ref[c, :] + second * other
            mixed = mixed_ref[:, c] + jnp.dot(
                q_ref[:, c], state.astype(BF16), preferred_element_type=F32
            )
            meansq = jnp.mean(mixed * mixed, axis=-1, keepdims=True)
            gain = gain_ref[:, pl.ds(pl.multiple_of(column + i * DH, DH), DH)]
            out_ref[m, :, c] = (mixed * lax.rsqrt(meansq + 1e-05) * gain).astype(BF16)
        store = pltpu.make_async_copy(out_ref.at[m], out_hbm.at[:, pl.ds(column, width)], sems.at[m])
        store.start()
        stores.append(store)
    for store in stores:
        store.wait()


def finish(gain, slots, out, width):
    places = list(slots)
    tokens = slots[places[0]][0].shape[0]
    earlier = [] if out is None else [out]
    operands = [gain]
    for q, mixed, state, from_core in slots.values():
        operands += [in_vmem(q), in_vmem(mixed), state, from_core]
    return pl.pallas_call(
        functools.partial(finish_kernel, places, width),
        in_specs=specs(*[pltpu.VMEM] * len(operands), *[pltpu.HBM] * len(earlier)),
        out_specs=specs(pltpu.HBM)[0],
        out_shape=jax.ShapeDtypeStruct((tokens, gain.shape[1]), BF16),
        scratch_shapes=[
            pltpu.VMEM((len(places), tokens, width), BF16),
            pltpu.SemaphoreType.DMA((len(places),)),
        ],
        input_output_aliases={len(operands): 0} if earlier else {},
        compiler_params=params(),
        cost_estimate=NO_COST,
        name="finish",
    )(*operands, *earlier)


def combine(compute, count, *operands):
    shape = operands[0].shape

    def kernel(*refs):
        ins, outs = refs[: len(operands)], refs[len(operands) :]
        core, chip = (a.astype(F32) for a in place())
        results = compute(core, chip, *[r[...] for r in ins])
        for ref, value in zip(outs, results):
            ref[...] = value

    results = pl.pallas_call(
        kernel,
        in_specs=specs(*[pltpu.VMEM] * len(operands)),
        out_specs=specs(*[pltpu.VMEM] * count),
        out_shape=[jax.ShapeDtypeStruct(shape, F32)] * count,
        compiler_params=params(),
        cost_estimate=NO_COST,
        name="combine",
    )(*operands)
    return list(results)


def send(name, array, axis, pairs):
    with jax.named_scope(name):
        return lax.ppermute(array, axis, pairs)


def add_to(core, chip, *arrays):
    *arrays, parts = arrays
    return [a + (parts[j] if parts.ndim == 3 else parts[j, 0]) for j, a in enumerate(arrays)]


def tie(*values):
    return lax.optimization_barrier(values)


def fast_path(q, k, v, gain, groups, heads_here):
    chunks = range(CHUNKS)
    width = heads_here // (4 * CHUNKS) * DH
    position = lax.axis_index("seq")
    core, chip = position % 2, position // 2
    where = jnp.stack([core, chip]).astype(jnp.int32)
    other_core = [(0, 1), (1, 0), (2, 3), (3, 2)]
    other_chip = [(0, 2), (2, 0), (1, 3), (3, 1)]

    sums, (lead, rest, q_lead) = kvsum(q, k, v, width)
    lead = send("lead", lead, "seq", other_core)
    there = combine(add_to, CHUNKS, *[s[1] for s in sums], lead)
    there[0], rest = tie(there[0], rest)
    rest = send("rest", rest, "seq", other_core)
    k_parts, v_parts = [s[2] for s in sums], [s[3] for s in sums]
    every = [(j, n) for j in chunks for n in range(4)]
    local, q_slots = [], None
    there[0], k_parts[0] = tie(there[0], k_parts[0])
    local, q_slots = local_slots(q, q_lead, None, k_parts, v_parts, width, every[:EARLY])
    q_slots = dict(zip(every, [q_lead, *q_slots]))
    from_chip = [send(f"chip{j}", t, "seq", other_chip) for j, t in enumerate(there)]
    from_chip[0], local = tie(from_chip[0], list(local))
    here = combine(add_to, CHUNKS, *[s[0] for s in sums], rest)
    group_total = [h + r for h, r in zip(here, from_chip)]

    arrived = [[] for _ in chunks]
    passing = group_total
    for hop in range(groups - 1):
        if hop == min(1, groups - 2):
            passing[-1], k_parts[0] = tie(passing[-1], k_parts[0])
            late, _ = local_slots(None, None, q_slots, k_parts, v_parts, width, every[len(local) :])
        received = [send(f"hop{hop}_{j}", p, "grp", [(hop, hop + 1)]) for j, p in enumerate(passing)]
        if hop == min(1, groups - 2):
            received[0], late = tie(received[0], late)
        for j in chunks:
            arrived[j].append(received[j])
        passing = [r + g for r, g in zip(received, group_total)]

    local = dict(zip(every, [*local, *late]))

    def turn(core, chip, here, from_chip, *arrived):
        before = sum(arrived[1:], arrived[0])
        return before + (1.0 - chip) * here, before + chip * from_chip

    turned = [combine(turn, 2, here[j], from_chip[j], *arrived[j]) for j in chunks]
    from_chip_back = [send(f"chipback{j}", t[0], "seq", other_chip) for j, t in enumerate(turned)]
    near_back = [send(f"near{j}", t[1], "seq", other_core) for j, t in enumerate(turned)]
    def early_slots(j):
        return {
            (j, 0): (q_slots[j, 0], local[j, 0], turned[j][1], rest),
            (j, 1): (q_slots[j, 1], local[j, 1], from_chip_back[j], lead),
            (j, 2): (q_slots[j, 2], local[j, 2], near_back[j], rest),
        }

    def last_slot(j):
        far_back = send(f"far{j}", from_chip_back[j], "seq", other_core)
        return {(j, 3): (q_slots[j, 3], local[j, 3], far_back, rest)}

    out, slots = None, {}
    for j in chunks:
        out = finish(gain, {**slots, **early_slots(j)}, out, width)
        slots = last_slot(j)
        if j + 1 < CHUNKS:
            from_chip_back[j + 1], out = tie(from_chip_back[j + 1], out)
    return finish(gain, slots, out, width)


def general_states(k, v, heads_here, nblocks, groups):
    def split(array):
        return array.reshape(nblocks, BLK, heads_here, DH)

    block_sums = jnp.einsum("bthd,bthe->bhde", split(k), split(v), preferred_element_type=F32)
    total = jnp.sum(block_sums, axis=0)
    earlier = jnp.concatenate([jnp.zeros_like(total)[None], jnp.cumsum(block_sums, axis=0)[:-1]])
    gathered = lax.all_gather(total, "seq")
    position = lax.axis_index("seq")
    lower = lax.broadcasted_iota(jnp.int32, (gathered.shape[0], 1, 1, 1), 0) < position
    within = jnp.sum(jnp.where(lower, gathered, 0.0), axis=0)
    group_total = jnp.sum(gathered, axis=0)
    before = jnp.zeros_like(total)
    passing = group_total
    for hop in range(groups - 1):
        received = lax.ppermute(passing, "grp", [(hop, hop + 1)])
        before = before + received
        passing = received + group_total
    return (before + within)[None] + earlier


def general_path(q, k, v, gain, groups, heads_here):
    tokens = q.shape[0]
    nblocks = tokens // BLK
    states = general_states(k, v, heads_here, nblocks, groups).astype(BF16)
    mixed = local_blocks(q, k, v, 1).reshape(nblocks, BLK, heads_here, DH)
    queries = q.reshape(nblocks, BLK, heads_here, DH)
    mixed = mixed + jnp.einsum("bthd,bhde->bthe", queries, states, preferred_element_type=F32)
    meansq = jnp.mean(mixed * mixed, axis=-1, keepdims=True)
    result = mixed * lax.rsqrt(meansq + 1e-05) * gain.reshape(heads_here, DH)
    return result.astype(BF16).reshape(q.shape)


def per_device(groups, shards, query_feat, key_feat, value_feat, norm_gain):
    shape = query_feat.shape
    tokens, width = shape[2:]
    heads_here = width // DH
    q, k, v = (a.reshape(tokens, width) for a in (query_feat, key_feat, value_feat))
    gain = norm_gain.reshape(1, width)
    fits = shards == 4 and groups > 1 and tokens == BLK and heads_here % (4 * CHUNKS) == 0
    path = fast_path if fits else general_path
    return path(q, k, v, gain, groups, heads_here).reshape(shape)


def solution(mesh):
    placed = P("grp", "seq", None, "head")
    return jax.shard_map(
        functools.partial(per_device, mesh.shape["grp"], mesh.shape["seq"]),
        mesh=mesh,
        in_specs=(placed, placed, placed, P("head")),
        out_specs=placed,
        check_vma=False,
    )
```

```python
import functools

import jax
import jax.numpy as jnp
from jax import lax
from jax.experimental import pallas as pl
from jax.experimental.pallas import tpu as pltpu
from jax.sharding import PartitionSpec as P

DH = 128
BLK = 512
TILE = 256
CHUNKS = 2
EARLY = 3
NO_COST = pl.CostEstimate(flops=0, bytes_accessed=0, transcendentals=0)
F32 = jnp.float32
BF16 = jnp.bfloat16
VMEM_LIMIT = 8 * 1024 * 1024


def params():
    return pltpu.CompilerParams(vmem_limit_bytes=VMEM_LIMIT)


def in_hbm(array):
    return pltpu.with_memory_space_constraint(array, pltpu.HBM)


def in_vmem(array):
    return pltpu.with_memory_space_constraint(array, pltpu.VMEM)


def head_cols(i):
    return slice(i * DH, (i + 1) * DH)


def slot_column(slot, width, core, chip):
    half = (slot // 2) ^ core
    quarter = (slot % 2) ^ chip
    return pl.multiple_of((half * 2 + quarter) * width, DH)


def place():
    position = lax.axis_index("seq")
    return position & 1, position >> 1


class Slots:
    def __init__(self, width):
        (self.core, self.chip), self.width = place(), width

    def column(self, first, slot):
        return pl.multiple_of(first + slot_column(slot, self.width, self.core, self.chip), DH)

    def load(self, first, slot, source, target, sem):
        copy = pltpu.make_async_copy(
            source.at[:, pl.ds(self.column(first, slot), self.width)], target, sem
        )
        copy.start()
        return copy


def specs(*spaces):
    return [pl.BlockSpec(memory_space=s) for s in spaces]


SLOT_ORDER = (3, 2, 0, 1)
KVSUM_OUTS = 4


def kvsum_kernel(width, k_hbm, v_hbm, *refs):
    *refs, lead, rest, sems = refs
    slots = Slots(width)
    outs = [refs[KVSUM_OUTS * j : KVSUM_OUTS * (j + 1)] for j in range(CHUNKS)]
    loads = []
    for slot in SLOT_ORDER:
        for j in range(CHUNKS):
            k_ref, v_ref = outs[j][2:]
            first = 4 * width * j
            loads.append(
                (
                    slot,
                    j,
                    slots.load(first, slot, k_hbm, k_ref.at[slot], sems.at[0, j, slot]),
                    slots.load(first, slot, v_hbm, v_ref.at[slot], sems.at[1, j, slot]),
                )
            )
    for slot, j, *copies in loads:
        for copy in copies:
            copy.wait()
        own, other, k_ref, v_ref = outs[j]
        for i in range(width // DH):
            c = head_cols(i)
            total = lax.dot_general(
                k_ref[slot, :, c],
                v_ref[slot, :, c],
                (((0,), (0,)), ((), ())),
                preferred_element_type=F32,
            )
            if slot == 3:
                lead[j, c, :] = total
            else:
                rest[j, (slot + 1) % 3, c, :] = total
            if slot < 2:
                (own, other)[slot][c, :] = total


def kvsum(k, v, width):
    tokens = k.shape[0]
    one = pltpu.VMEM((width, DH), F32)
    part = pltpu.VMEM((4, tokens, width), BF16)
    outs = [one, one, part, part] * CHUNKS
    outs += [pltpu.VMEM((CHUNKS, width, DH), F32), pltpu.VMEM((CHUNKS, 3, width, DH), F32)]
    results = pl.pallas_call(
        functools.partial(kvsum_kernel, width),
        in_specs=specs(pltpu.HBM, pltpu.HBM),
        out_specs=specs(*[pltpu.VMEM] * len(outs)),
        out_shape=outs,
        scratch_shapes=[pltpu.SemaphoreType.DMA((2, CHUNKS, 4))],
        compiler_params=params(),
        cost_estimate=NO_COST,
        name="kvsum",
    )(in_hbm(k), in_hbm(v))
    return [results[KVSUM_OUTS * j : KVSUM_OUTS * (j + 1)] for j in range(CHUNKS)], results[-2:]


def local_scores(q_ref, k_ref, c):
    rows = lax.broadcasted_iota(jnp.int32, (TILE, TILE), 0)
    cols = lax.broadcasted_iota(jnp.int32, (TILE, TILE), 1)
    causal = rows >= cols
    tiles = []
    for t in range(BLK // TILE):
        scores = lax.dot_general(
            q_ref[t * TILE : (t + 1) * TILE, c],
            k_ref[: (t + 1) * TILE, c],
            (((1,), (1,)), ((), ())),
            preferred_element_type=F32,
        )
        last = jnp.where(causal, scores[:, t * TILE :], 0.0).astype(BF16)
        if t > 0:
            last = jnp.concatenate([scores[:, : t * TILE].astype(BF16), last], axis=1)
        tiles.append(last)
    return tiles


def local_mix(tiles, v_ref, out_ref, c):
    for t, scores in enumerate(tiles):
        out_ref[t * TILE : (t + 1) * TILE, c] = jnp.dot(
            scores, v_ref[: (t + 1) * TILE, c], preferred_element_type=F32
        )


def local_heads(items):
    held = None
    for q_ref, k_ref, v_ref, out_ref, c in items:
        tiles = local_scores(q_ref, k_ref, c)
        if held is not None:
            local_mix(*held)
        held = (tiles, v_ref, out_ref, c)
    local_mix(*held)


def local_kernel(heads, q_ref, k_ref, v_ref, mixed_ref):
    local_heads([(q_ref, k_ref, v_ref, mixed_ref, head_cols(i)) for i in range(heads)])


def local_blocks(q, k, v, heads):
    tokens, width = q.shape
    spec = pl.BlockSpec((BLK, heads * DH), lambda b, s: (b, s))
    return pl.pallas_call(
        functools.partial(local_kernel, heads),
        grid=(tokens // BLK, width // (heads * DH)),
        in_specs=[spec] * 3,
        out_specs=spec,
        out_shape=jax.ShapeDtypeStruct((tokens, width), F32),
        compiler_params=params(),
        name="local_attention",
    )(q, k, v)


def local_slots_kernel(width, places, load, *refs):
    count = len(places)
    if load:
        every = [(j, n) for j in range(CHUNKS) for n in range(4)]
        q_hbm, *refs, sems = refs
        q_refs, refs = dict(zip(every, refs[-len(every) :])), refs[: -len(every)]
        slots = Slots(width)
        loads = {
            (j, n): slots.load(4 * width * j, n, q_hbm, q_refs[j, n], sems.at[j, n]) for j, n in every
        }
    else:
        q_refs, loads, refs = dict(zip(places, refs)), {}, refs[count:]
    k_refs, v_refs, out_refs = refs[:CHUNKS], refs[CHUNKS : 2 * CHUNKS], refs[2 * CHUNKS :]

    def items():
        for place, out_ref in zip(places, out_refs):
            j, n = place
            if place in loads:
                loads.pop(place).wait()
            for i in range(width // DH):
                yield q_refs[place], k_refs[j].at[n], v_refs[j].at[n], out_ref, head_cols(i)

    local_heads(items())
    for copy in loads.values():
        copy.wait()


def local_slots(q, q_slots, k_parts, v_parts, width, places):
    tokens = k_parts[0].shape[1]
    load = q_slots is None
    every = 4 * CHUNKS
    queries = [] if load else [q_slots[p] for p in places]
    outs = [pltpu.VMEM((tokens, width), F32)] * len(places)
    outs += [pltpu.VMEM((tokens, width), BF16)] * (every * load)
    results = pl.pallas_call(
        functools.partial(local_slots_kernel, width, places, load),
        in_specs=specs(*[pltpu.HBM] * load, *[pltpu.VMEM] * (len(queries) + 2 * CHUNKS)),
        out_specs=specs(*[pltpu.VMEM] * len(outs)),
        out_shape=outs,
        scratch_shapes=[pltpu.SemaphoreType.DMA((CHUNKS, 4))] * load,
        compiler_params=params(),
        cost_estimate=NO_COST,
        name="local_attention",
    )(*([in_hbm(q)] if load else []), *[in_vmem(a) for a in (*queries, *k_parts, *v_parts)])
    return results[: len(places)], results[len(places) :]


def finish_kernel(places, width, gain_ref, *refs):
    out_hbm, out_ref, sems = refs[-3:]
    slots = Slots(width)
    second = slots.core.astype(F32)
    stores = []
    for m, (j, n) in enumerate(places):
        q_ref, mixed_ref, state_ref, from_core = refs[4 * m : 4 * m + 4]
        column = slots.column(4 * width * j, n)
        for i in range(width // DH):
            c = head_cols(i)
            other = from_core[j, c, :] if n == 1 else from_core[j, max(n - 1, 0), c, :]
            state = state_ref[c, :] + second * other
            mixed = mixed_ref[:, c] + jnp.dot(
                q_ref[:, c], state.astype(BF16), preferred_element_type=F32
            )
            meansq = jnp.mean(mixed * mixed, axis=-1, keepdims=True)
            gain = gain_ref[:, pl.ds(pl.multiple_of(column + i * DH, DH), DH)]
            out_ref[m, :, c] = (mixed * lax.rsqrt(meansq + 1e-05) * gain).astype(BF16)
        store = pltpu.make_async_copy(out_ref.at[m], out_hbm.at[:, pl.ds(column, width)], sems.at[m])
        store.start()
        stores.append(store)
    for store in stores:
        store.wait()


def finish(gain, slots, out, width):
    places = list(slots)
    tokens = slots[places[0]][0].shape[0]
    earlier = [] if out is None else [out]
    operands = [gain]
    for q, mixed, state, from_core in slots.values():
        operands += [in_vmem(q), in_vmem(mixed), state, from_core]
    return pl.pallas_call(
        functools.partial(finish_kernel, places, width),
        in_specs=specs(*[pltpu.VMEM] * len(operands), *[pltpu.HBM] * len(earlier)),
        out_specs=specs(pltpu.HBM)[0],
        out_shape=jax.ShapeDtypeStruct((tokens, gain.shape[1]), BF16),
        scratch_shapes=[
            pltpu.VMEM((len(places), tokens, width), BF16),
            pltpu.SemaphoreType.DMA((len(places),)),
        ],
        input_output_aliases={len(operands): 0} if earlier else {},
        compiler_params=params(),
        cost_estimate=NO_COST,
        name="finish",
    )(*operands, *earlier)


def combine(compute, count, *operands):
    shape = operands[0].shape

    def kernel(*refs):
        ins, outs = refs[: len(operands)], refs[len(operands) :]
        core, chip = (a.astype(F32) for a in place())
        results = compute(core, chip, *[r[...] for r in ins])
        for ref, value in zip(outs, results):
            ref[...] = value

    results = pl.pallas_call(
        kernel,
        in_specs=specs(*[pltpu.VMEM] * len(operands)),
        out_specs=specs(*[pltpu.VMEM] * count),
        out_shape=[jax.ShapeDtypeStruct(shape, F32)] * count,
        compiler_params=params(),
        cost_estimate=NO_COST,
        name="combine",
    )(*operands)
    return list(results)


def send(name, array, axis, pairs):
    with jax.named_scope(name):
        return lax.ppermute(array, axis, pairs)


def add_to(core, chip, *arrays):
    *arrays, parts = arrays
    return [a + (parts[j] if parts.ndim == 3 else parts[j, 0]) for j, a in enumerate(arrays)]


def tie(*values):
    return lax.optimization_barrier(values)


def fast_path(q, k, v, gain, groups, heads_here):
    chunks = range(CHUNKS)
    width = heads_here // (4 * CHUNKS) * DH
    position = lax.axis_index("seq")
    core, chip = position % 2, position // 2
    where = jnp.stack([core, chip]).astype(jnp.int32)
    other_core = [(0, 1), (1, 0), (2, 3), (3, 2)]
    other_chip = [(0, 2), (2, 0), (1, 3), (3, 1)]

    sums, (lead, rest) = kvsum(k, v, width)
    lead = send("lead", lead, "seq", other_core)
    there = combine(add_to, CHUNKS, *[s[1] for s in sums], lead)
    there[0], rest = tie(there[0], rest)
    rest = send("rest", rest, "seq", other_core)
    k_parts, v_parts = [s[2] for s in sums], [s[3] for s in sums]
    every = [(j, n) for j in chunks for n in range(4)]
    local, q_slots = [], None
    there[0], k_parts[0] = tie(there[0], k_parts[0])
    local, q_slots = local_slots(q, None, k_parts, v_parts, width, every[:EARLY])
    q_slots = dict(zip(every, q_slots))
    from_chip = [send(f"chip{j}", t, "seq", other_chip) for j, t in enumerate(there)]
    from_chip[0], local = tie(from_chip[0], list(local))
    here = combine(add_to, CHUNKS, *[s[0] for s in sums], rest)
    group_total = [h + r for h, r in zip(here, from_chip)]

    arrived = [[] for _ in chunks]
    passing = group_total
    for hop in range(groups - 1):
        if hop == min(1, groups - 2):
            passing[-1], k_parts[0] = tie(passing[-1], k_parts[0])
            late, _ = local_slots(None, q_slots, k_parts, v_parts, width, every[len(local) :])
        received = [send(f"hop{hop}_{j}", p, "grp", [(hop, hop + 1)]) for j, p in enumerate(passing)]
        if hop == min(1, groups - 2):
            received[0], late = tie(received[0], late)
        for j in chunks:
            arrived[j].append(received[j])
        passing = [r + g for r, g in zip(received, group_total)]

    local = dict(zip(every, [*local, *late]))

    def turn(core, chip, here, from_chip, *arrived):
        before = sum(arrived[1:], arrived[0])
        return before + (1.0 - chip) * here, before + chip * from_chip

    turned = [combine(turn, 2, here[j], from_chip[j], *arrived[j]) for j in chunks]
    from_chip_back = [send(f"chipback{j}", t[0], "seq", other_chip) for j, t in enumerate(turned)]
    near_back = [send(f"near{j}", t[1], "seq", other_core) for j, t in enumerate(turned)]
    def early_slots(j):
        return {
            (j, 0): (q_slots[j, 0], local[j, 0], turned[j][1], rest),
            (j, 1): (q_slots[j, 1], local[j, 1], from_chip_back[j], lead),
            (j, 2): (q_slots[j, 2], local[j, 2], near_back[j], rest),
        }

    def last_slot(j):
        far_back = send(f"far{j}", from_chip_back[j], "seq", other_core)
        return {(j, 3): (q_slots[j, 3], local[j, 3], far_back, rest)}

    out, slots = None, {}
    for j in chunks:
        out = finish(gain, {**slots, **early_slots(j)}, out, width)
        slots = last_slot(j)
        if j + 1 < CHUNKS:
            from_chip_back[j + 1], out = tie(from_chip_back[j + 1], out)
    return finish(gain, slots, out, width)


def general_states(k, v, heads_here, nblocks, groups):
    def split(array):
        return array.reshape(nblocks, BLK, heads_here, DH)

    block_sums = jnp.einsum("bthd,bthe->bhde", split(k), split(v), preferred_element_type=F32)
    total = jnp.sum(block_sums, axis=0)
    earlier = jnp.concatenate([jnp.zeros_like(total)[None], jnp.cumsum(block_sums, axis=0)[:-1]])
    gathered = lax.all_gather(total, "seq")
    position = lax.axis_index("seq")
    lower = lax.broadcasted_iota(jnp.int32, (gathered.shape[0], 1, 1, 1), 0) < position
    within = jnp.sum(jnp.where(lower, gathered, 0.0), axis=0)
    group_total = jnp.sum(gathered, axis=0)
    before = jnp.zeros_like(total)
    passing = group_total
    for hop in range(groups - 1):
        received = lax.ppermute(passing, "grp", [(hop, hop + 1)])
        before = before + received
        passing = received + group_total
    return (before + within)[None] + earlier


def general_path(q, k, v, gain, groups, heads_here):
    tokens = q.shape[0]
    nblocks = tokens // BLK
    states = general_states(k, v, heads_here, nblocks, groups).astype(BF16)
    mixed = local_blocks(q, k, v, 1).reshape(nblocks, BLK, heads_here, DH)
    queries = q.reshape(nblocks, BLK, heads_here, DH)
    mixed = mixed + jnp.einsum("bthd,bhde->bthe", queries, states, preferred_element_type=F32)
    meansq = jnp.mean(mixed * mixed, axis=-1, keepdims=True)
    result = mixed * lax.rsqrt(meansq + 1e-05) * gain.reshape(heads_here, DH)
    return result.astype(BF16).reshape(q.shape)


def per_device(groups, shards, query_feat, key_feat, value_feat, norm_gain):
    shape = query_feat.shape
    tokens, width = shape[2:]
    heads_here = width // DH
    q, k, v = (a.reshape(tokens, width) for a in (query_feat, key_feat, value_feat))
    gain = norm_gain.reshape(1, width)
    fits = shards == 4 and groups > 1 and tokens == BLK and heads_here % (4 * CHUNKS) == 0
    path = fast_path if fits else general_path
    return path(q, k, v, gain, groups, heads_here).reshape(shape)


def solution(mesh):
    placed = P("grp", "seq", None, "head")
    return jax.shard_map(
        functools.partial(per_device, mesh.shape["grp"], mesh.shape["seq"]),
        mesh=mesh,
        in_specs=(placed, placed, placed, P("head")),
        out_specs=placed,
        check_vma=False,
    )
```

```python
import functools

import jax
import jax.numpy as jnp
from jax import lax
from jax.experimental import pallas as pl
from jax.experimental.pallas import tpu as pltpu
from jax.sharding import PartitionSpec as P

DH = 128
BLK = 512
TILE = 256
CHUNKS = 2
EARLY = 3
NO_COST = pl.CostEstimate(flops=0, bytes_accessed=0, transcendentals=0)
F32 = jnp.float32
BF16 = jnp.bfloat16
VMEM_LIMIT = 8 * 1024 * 1024


def params():
    return pltpu.CompilerParams(vmem_limit_bytes=VMEM_LIMIT)


def in_hbm(array):
    return pltpu.with_memory_space_constraint(array, pltpu.HBM)


def in_vmem(array):
    return pltpu.with_memory_space_constraint(array, pltpu.VMEM)


def head_cols(i):
    return slice(i * DH, (i + 1) * DH)


def slot_column(slot, width, core, chip):
    half = (slot // 2) ^ core
    quarter = (slot % 2) ^ chip
    return pl.multiple_of((half * 2 + quarter) * width, DH)


def place():
    position = lax.axis_index("seq")
    return position & 1, position >> 1


class Slots:
    def __init__(self, width):
        (self.core, self.chip), self.width = place(), width

    def column(self, first, slot):
        return pl.multiple_of(first + slot_column(slot, self.width, self.core, self.chip), DH)

    def load(self, first, slot, source, target, sem):
        copy = pltpu.make_async_copy(
            source.at[:, pl.ds(self.column(first, slot), self.width)], target, sem
        )
        copy.start()
        return copy


def specs(*spaces):
    return [pl.BlockSpec(memory_space=s) for s in spaces]


SLOT_ORDER = (3, 2, 0, 1)
KVSUM_OUTS = 4


def kvsum_kernel(width, k_hbm, v_hbm, *refs):
    *refs, lead, rest, sems = refs
    slots = Slots(width)
    outs = [refs[KVSUM_OUTS * j : KVSUM_OUTS * (j + 1)] for j in range(CHUNKS)]
    loads = []
    for slot in SLOT_ORDER:
        for j in range(CHUNKS):
            k_ref, v_ref = outs[j][2:]
            first = 4 * width * j
            loads.append(
                (
                    slot,
                    j,
                    slots.load(first, slot, k_hbm, k_ref.at[slot], sems.at[0, j, slot]),
                    slots.load(first, slot, v_hbm, v_ref.at[slot], sems.at[1, j, slot]),
                )
            )
    for slot, j, *copies in loads:
        for copy in copies:
            copy.wait()
        own, other, k_ref, v_ref = outs[j]
        for i in range(width // DH):
            c = head_cols(i)
            total = lax.dot_general(
                k_ref[slot, :, c],
                v_ref[slot, :, c],
                (((0,), (0,)), ((), ())),
                preferred_element_type=F32,
            )
            if slot == 3:
                lead[j, c, :] = total
            else:
                rest[j, (slot + 1) % 3, c, :] = total
            if slot < 2:
                (own, other)[slot][c, :] = total


def kvsum(k, v, width):
    tokens = k.shape[0]
    one = pltpu.VMEM((width, DH), F32)
    part = pltpu.VMEM((4, tokens, width), BF16)
    outs = [one, one, part, part] * CHUNKS
    outs += [pltpu.VMEM((CHUNKS, width, DH), F32), pltpu.VMEM((CHUNKS, 3, width, DH), F32)]
    results = pl.pallas_call(
        functools.partial(kvsum_kernel, width),
        in_specs=specs(pltpu.HBM, pltpu.HBM),
        out_specs=specs(*[pltpu.VMEM] * len(outs)),
        out_shape=outs,
        scratch_shapes=[pltpu.SemaphoreType.DMA((2, CHUNKS, 4))],
        compiler_params=params(),
        cost_estimate=NO_COST,
        name="kvsum",
    )(in_hbm(k), in_hbm(v))
    return [results[KVSUM_OUTS * j : KVSUM_OUTS * (j + 1)] for j in range(CHUNKS)], results[-2:]


def local_scores(q_ref, k_ref, c):
    rows = lax.broadcasted_iota(jnp.int32, (TILE, TILE), 0)
    cols = lax.broadcasted_iota(jnp.int32, (TILE, TILE), 1)
    causal = rows >= cols
    tiles = []
    for t in range(BLK // TILE):
        scores = lax.dot_general(
            q_ref[t * TILE : (t + 1) * TILE, c],
            k_ref[: (t + 1) * TILE, c],
            (((1,), (1,)), ((), ())),
            preferred_element_type=F32,
        )
        last = jnp.where(causal, scores[:, t * TILE :], 0.0).astype(BF16)
        if t > 0:
            last = jnp.concatenate([scores[:, : t * TILE].astype(BF16), last], axis=1)
        tiles.append(last)
    return tiles


def local_mix(tiles, v_ref, out_ref, c):
    for t, scores in enumerate(tiles):
        out_ref[t * TILE : (t + 1) * TILE, c] = jnp.dot(
            scores, v_ref[: (t + 1) * TILE, c], preferred_element_type=F32
        )


def local_heads(items):
    held = None
    for q_ref, k_ref, v_ref, out_ref, c in items:
        tiles = local_scores(q_ref, k_ref, c)
        if held is not None:
            local_mix(*held)
        held = (tiles, v_ref, out_ref, c)
    local_mix(*held)


def local_kernel(heads, q_ref, k_ref, v_ref, mixed_ref):
    local_heads([(q_ref, k_ref, v_ref, mixed_ref, head_cols(i)) for i in range(heads)])


def local_blocks(q, k, v, heads):
    tokens, width = q.shape
    spec = pl.BlockSpec((BLK, heads * DH), lambda b, s: (b, s))
    return pl.pallas_call(
        functools.partial(local_kernel, heads),
        grid=(tokens // BLK, width // (heads * DH)),
        in_specs=[spec] * 3,
        out_specs=spec,
        out_shape=jax.ShapeDtypeStruct((tokens, width), F32),
        compiler_params=params(),
        name="local_attention",
    )(q, k, v)


def local_slots_kernel(width, places, load, *refs):
    count = len(places)
    if load:
        every = [(j, n) for j in range(CHUNKS) for n in range(4)]
        q_hbm, *refs, sems = refs
        q_refs, refs = dict(zip(every, refs[-len(every) :])), refs[: -len(every)]
        slots = Slots(width)
        loads = {
            (j, n): slots.load(4 * width * j, n, q_hbm, q_refs[j, n], sems.at[j, n]) for j, n in every
        }
    else:
        q_refs, loads, refs = dict(zip(places, refs)), {}, refs[count:]
    k_refs, v_refs, out_refs = refs[:CHUNKS], refs[CHUNKS : 2 * CHUNKS], refs[2 * CHUNKS :]

    def items():
        for place, out_ref in zip(places, out_refs):
            j, n = place
            if place in loads:
                loads.pop(place).wait()
            for i in range(width // DH):
                yield q_refs[place], k_refs[j].at[n], v_refs[j].at[n], out_ref, head_cols(i)

    local_heads(items())
    for copy in loads.values():
        copy.wait()


def local_slots(q, q_slots, k_parts, v_parts, width, places):
    tokens = k_parts[0].shape[1]
    load = q_slots is None
    every = 4 * CHUNKS
    queries = [] if load else [q_slots[p] for p in places]
    outs = [pltpu.VMEM((tokens, width), F32)] * len(places)
    outs += [pltpu.VMEM((tokens, width), BF16)] * (every * load)
    results = pl.pallas_call(
        functools.partial(local_slots_kernel, width, places, load),
        in_specs=specs(*[pltpu.HBM] * load, *[pltpu.VMEM] * (len(queries) + 2 * CHUNKS)),
        out_specs=specs(*[pltpu.VMEM] * len(outs)),
        out_shape=outs,
        scratch_shapes=[pltpu.SemaphoreType.DMA((CHUNKS, 4))] * load,
        compiler_params=params(),
        cost_estimate=NO_COST,
        name="local_attention",
    )(*([in_hbm(q)] if load else []), *[in_vmem(a) for a in (*queries, *k_parts, *v_parts)])
    return results[: len(places)], results[len(places) :]


def finish_kernel(places, width, gain_ref, *refs):
    out_hbm, out_ref, sems = refs[-3:]
    slots = Slots(width)
    second = slots.core.astype(F32)
    stores = []
    for m, (j, n) in enumerate(places):
        q_ref, mixed_ref, state_ref, from_core = refs[4 * m : 4 * m + 4]
        column = slots.column(4 * width * j, n)
        for i in range(width // DH):
            c = head_cols(i)
            other = from_core[j, c, :] if n == 1 else from_core[j, max(n - 1, 0), c, :]
            state = state_ref[c, :] + second * other
            mixed = mixed_ref[:, c] + jnp.dot(
                q_ref[:, c], state.astype(BF16), preferred_element_type=F32
            )
            meansq = jnp.mean(mixed * mixed, axis=-1, keepdims=True)
            gain = gain_ref[:, pl.ds(pl.multiple_of(column + i * DH, DH), DH)]
            out_ref[m, :, c] = (mixed * lax.rsqrt(meansq + 1e-05) * gain).astype(BF16)
        store = pltpu.make_async_copy(out_ref.at[m], out_hbm.at[:, pl.ds(column, width)], sems.at[m])
        store.start()
        stores.append(store)
    for store in stores:
        store.wait()


def finish(gain, slots, out, width):
    places = list(slots)
    tokens = slots[places[0]][0].shape[0]
    earlier = [] if out is None else [out]
    operands = [gain]
    for q, mixed, state, from_core in slots.values():
        operands += [in_vmem(q), in_vmem(mixed), state, from_core]
    return pl.pallas_call(
        functools.partial(finish_kernel, places, width),
        in_specs=specs(*[pltpu.VMEM] * len(operands), *[pltpu.HBM] * len(earlier)),
        out_specs=specs(pltpu.HBM)[0],
        out_shape=jax.ShapeDtypeStruct((tokens, gain.shape[1]), BF16),
        scratch_shapes=[
            pltpu.VMEM((len(places), tokens, width), BF16),
            pltpu.SemaphoreType.DMA((len(places),)),
        ],
        input_output_aliases={len(operands): 0} if earlier else {},
        compiler_params=params(),
        cost_estimate=NO_COST,
        name="finish",
    )(*operands, *earlier)


def combine(compute, count, *operands):
    shape = operands[0].shape

    def kernel(*refs):
        ins, outs = refs[: len(operands)], refs[len(operands) :]
        core, chip = (a.astype(F32) for a in place())
        results = compute(core, chip, *[r[...] for r in ins])
        for ref, value in zip(outs, results):
            ref[...] = value

    results = pl.pallas_call(
        kernel,
        in_specs=specs(*[pltpu.VMEM] * len(operands)),
        out_specs=specs(*[pltpu.VMEM] * count),
        out_shape=[jax.ShapeDtypeStruct(shape, F32)] * count,
        compiler_params=params(),
        cost_estimate=NO_COST,
        name="combine",
    )(*operands)
    return list(results)


def send(name, array, axis, pairs):
    with jax.named_scope(name):
        return lax.ppermute(array, axis, pairs)


def add_to(core, chip, *arrays):
    *arrays, parts = arrays
    return [a + (parts[j] if parts.ndim == 3 else parts[j, 0]) for j, a in enumerate(arrays)]


def tie(*values):
    return lax.optimization_barrier(values)


def fast_path(q, k, v, gain, groups, heads_here):
    chunks = range(CHUNKS)
    width = heads_here // (4 * CHUNKS) * DH
    position = lax.axis_index("seq")
    core, chip = position % 2, position // 2
    where = jnp.stack([core, chip]).astype(jnp.int32)
    other_core = [(0, 1), (1, 0), (2, 3), (3, 2)]
    other_chip = [(0, 2), (2, 0), (1, 3), (3, 1)]

    sums, (lead, rest) = kvsum(k, v, width)
    lead = send("lead", lead, "seq", other_core)
    there = combine(add_to, CHUNKS, *[s[1] for s in sums], lead)
    there[0], rest = tie(there[0], rest)
    rest = send("rest", rest, "seq", other_core)
    k_parts, v_parts = [s[2] for s in sums], [s[3] for s in sums]
    every = [(j, n) for j in chunks for n in range(4)]
    local, q_slots = [], None
    there[0], k_parts[0] = tie(there[0], k_parts[0])
    local, q_slots = local_slots(q, None, k_parts, v_parts, width, every[:EARLY])
    q_slots = dict(zip(every, q_slots))
    from_chip = [send(f"chip{j}", t, "seq", other_chip) for j, t in enumerate(there)]
    from_chip[0], local = tie(from_chip[0], list(local))
    here = combine(add_to, CHUNKS, *[s[0] for s in sums], rest)
    group_total = [h + r for h, r in zip(here, from_chip)]

    arrived = [[] for _ in chunks]
    passing = group_total
    for hop in range(groups - 1):
        if hop == min(1, groups - 2):
            passing[0], k_parts[0] = tie(passing[0], k_parts[0])
            late, _ = local_slots(None, q_slots, k_parts, v_parts, width, every[len(local) :])
        received = [send(f"hop{hop}_{j}", p, "grp", [(hop, hop + 1)]) for j, p in enumerate(passing)]
        if hop == min(1, groups - 2):
            received[0], late = tie(received[0], late)
        for j in chunks:
            arrived[j].append(received[j])
        passing = [r + g for r, g in zip(received, group_total)]

    local = dict(zip(every, [*local, *late]))

    def turn(core, chip, here, from_chip, *arrived):
        before = sum(arrived[1:], arrived[0])
        return before + (1.0 - chip) * here, before + chip * from_chip

    turned = [combine(turn, 2, here[j], from_chip[j], *arrived[j]) for j in chunks]
    from_chip_back = [send(f"chipback{j}", t[0], "seq", other_chip) for j, t in enumerate(turned)]
    near_back = [send(f"near{j}", t[1], "seq", other_core) for j, t in enumerate(turned)]
    def early_slots(j):
        return {
            (j, 0): (q_slots[j, 0], local[j, 0], turned[j][1], rest),
            (j, 1): (q_slots[j, 1], local[j, 1], from_chip_back[j], lead),
            (j, 2): (q_slots[j, 2], local[j, 2], near_back[j], rest),
        }

    def last_slot(j):
        far_back = send(f"far{j}", from_chip_back[j], "seq", other_core)
        return {(j, 3): (q_slots[j, 3], local[j, 3], far_back, rest)}

    out, slots = None, {}
    for j in chunks:
        out = finish(gain, {**slots, **early_slots(j)}, out, width)
        slots = last_slot(j)
        if j + 1 < CHUNKS:
            from_chip_back[j + 1], out = tie(from_chip_back[j + 1], out)
    return finish(gain, slots, out, width)


def general_states(k, v, heads_here, nblocks, groups):
    def split(array):
        return array.reshape(nblocks, BLK, heads_here, DH)

    block_sums = jnp.einsum("bthd,bthe->bhde", split(k), split(v), preferred_element_type=F32)
    total = jnp.sum(block_sums, axis=0)
    earlier = jnp.concatenate([jnp.zeros_like(total)[None], jnp.cumsum(block_sums, axis=0)[:-1]])
    gathered = lax.all_gather(total, "seq")
    position = lax.axis_index("seq")
    lower = lax.broadcasted_iota(jnp.int32, (gathered.shape[0], 1, 1, 1), 0) < position
    within = jnp.sum(jnp.where(lower, gathered, 0.0), axis=0)
    group_total = jnp.sum(gathered, axis=0)
    before = jnp.zeros_like(total)
    passing = group_total
    for hop in range(groups - 1):
        received = lax.ppermute(passing, "grp", [(hop, hop + 1)])
        before = before + received
        passing = received + group_total
    return (before + within)[None] + earlier


def general_path(q, k, v, gain, groups, heads_here):
    tokens = q.shape[0]
    nblocks = tokens // BLK
    states = general_states(k, v, heads_here, nblocks, groups).astype(BF16)
    mixed = local_blocks(q, k, v, 1).reshape(nblocks, BLK, heads_here, DH)
    queries = q.reshape(nblocks, BLK, heads_here, DH)
    mixed = mixed + jnp.einsum("bthd,bhde->bthe", queries, states, preferred_element_type=F32)
    meansq = jnp.mean(mixed * mixed, axis=-1, keepdims=True)
    result = mixed * lax.rsqrt(meansq + 1e-05) * gain.reshape(heads_here, DH)
    return result.astype(BF16).reshape(q.shape)


def per_device(groups, shards, query_feat, key_feat, value_feat, norm_gain):
    shape = query_feat.shape
    tokens, width = shape[2:]
    heads_here = width // DH
    q, k, v = (a.reshape(tokens, width) for a in (query_feat, key_feat, value_feat))
    gain = norm_gain.reshape(1, width)
    fits = shards == 4 and groups > 1 and tokens == BLK and heads_here % (4 * CHUNKS) == 0
    path = fast_path if fits else general_path
    return path(q, k, v, gain, groups, heads_here).reshape(shape)


def solution(mesh):
    placed = P("grp", "seq", None, "head")
    return jax.shard_map(
        functools.partial(per_device, mesh.shape["grp"], mesh.shape["seq"]),
        mesh=mesh,
        in_specs=(placed, placed, placed, P("head")),
        out_specs=placed,
        check_vma=False,
    )
```
